32 devices in a mesh: lat: 4 (over x, core), lon: 8 (over z, y).
Axes of the slice: x: 2, y: 2, z: 4, core: 2. Of those that a mesh axis runs over, the one named last changes fastest.
Arguments:
- cell_state: bfloat16 [4, 8, 512, 32, 64], P('lat', 'lon'), may hold values from -6 to 6
- remap_weight: bfloat16 [4, 8, 512, 64, 128], P('lat', 'lon'), may hold values from -0.75 to 0.75
- block_target: int32 [4, 8, 512], P('lat', 'lon'), may hold values from 0 to 255, as said below
- block_count: int32 [4, 8], P('lat', 'lon'), may hold values from 256 to 512, as said below
- border_state: bfloat16 [4, 8, 128, 32, 64], P('lat', 'lon'), may hold values from -6 to 6
- border_weight: bfloat16 [4, 8, 128, 64, 128], P('lat', 'lon'), may hold values from -0.75 to 0.75
- border_target: int32 [4, 8, 128], P('lat', 'lon'), may hold values from 0 to 63
- kernel_one: bfloat16 [7, 7, 32, 64], replicated, may hold values from -0.15625 to 0.15625
- bias_one: float32 [64], replicated, may hold values from -4 to 4
- gain_one: float32 [64], replicated, may hold values from 0.1 to 1.9
- kernel_two: bfloat16 [7, 7, 64, 128], replicated, may hold values from -0.109375 to 0.109375
- bias_two: float32 [128], replicated, may hold values from -4 to 4
- gain_two: float32 [128], replicated, may hold values from 0.1 to 1.9
Outputs:
- encoded: bfloat16 [256, 256, 128], P('lat', 'lon')
The draws below stay inside these ranges and needn't reach their ends.
Inputs may be any that keep to these rules, and one draw needn't show every extreme that they name: `block_count`: slots below a device's count are live; the largest count is exactly 512 in every draw. `block_target`: on every device, slots 0 to 255 name each patch of the tile once, in an order drawn from the seed; later slots name patches at random.
All inputs are finite; a program needn't handle non-finite values.
Results may differ from the reference program's by a relative error of at most 0.0045.
Values may be sent and summed in bfloat16 or wider, within the bound.
A program may use at most 192 MiB of HBM per device.

```python
import jax
import jax.numpy as jnp
from jax import lax

C = 32
C1 = 64
C2 = 128
BC = 64
PH = 8
PW = 16
EDGE = 1
TH = 256
W = 128
NB = 512
P_SIZE = 128
PR = 32
PC = 8
NP = 256
EP = 32
NS = 128
BANDS = 4
SECTORS = 8
ROWS = 1024
COLS = 1024


def draw_block_count(key, part):
    band_no = jnp.arange(BANDS, dtype=jnp.int32)[:, None] + jnp.zeros((1, SECTORS), jnp.int32)
    is_polar = (band_no == 0) | (band_no == BANDS - 1)
    spread = NB - NP
    factors = jax.random.randint(jax.random.fold_in(key, 11), (3, BANDS, SECTORS), 0, 9)
    extra_slots = factors[0] * factors[1] * factors[2] * spread // 512
    polar_extra = factors[0] * (spread // 8) // 8
    counts = NP + jnp.where(is_polar, polar_extra, extra_slots)
    return counts.at[BANDS // 2, 0].set(NB).astype(jnp.int32)


def draw_block_target(key, part):
    key_list = jax.random.split(jax.random.fold_in(key, 23), BANDS * SECTORS)
    orders = jax.vmap(lambda one_key: jax.random.permutation(one_key, NP))(key_list)
    remaining = jax.random.randint(jax.random.fold_in(key, 29), (BANDS * SECTORS, NB - NP), 0, NP)
    joined = jnp.concatenate([orders.astype(jnp.int32), remaining.astype(jnp.int32)], 1)
    return joined.reshape(BANDS, SECTORS, NB)


def set_ends(result, own_key, least, top_value):
    extent = result.shape
    spot = [jax.random.randint(jax.random.fold_in(own_key, axis), (), 0, extent[axis]) for axis in range(len(extent))]
    result = result.at[tuple(spot)].set(least)
    longest = extent.index(max(extent))
    spot[longest] = (spot[longest] + 1) % extent[longest]
    return result.at[tuple(spot)].set(top_value)


def level_of(stream_key, shape, cuts, low, largest):
    def one(dim, parts):
        heights = jax.random.uniform(jax.random.fold_in(jax.random.fold_in(stream_key, 6), dim), (parts,), jnp.float32, low / len(cuts), largest / len(cuts))
        return jnp.repeat(jnp.exp(heights), shape[dim] // parts).reshape((-1,) + (1,) * (len(shape) - dim - 1))

    factor_of = one(*cuts[0])
    for cut in cuts[1:]:
        factor_of = factor_of * one(*cut)
    return factor_of


def noise(own_key, dims, deviation, reach, cuts=(), kind=jnp.bfloat16):
    values = deviation * jax.random.normal(own_key, dims, jnp.float32)
    if cuts:
        values = values * level_of(own_key, dims, cuts, -0.22, 0.18)
    return jnp.clip(values, -reach, reach).astype(kind)


def setup_inputs(seed: int = 0) -> dict:
    splits = jax.random.split(jax.random.key(seed), 14)
    cell_state = noise(splits[0], (BANDS, SECTORS, NB, C, BC), 1.0, 6.0, ((0, 4), (1, 8)))
    remap_weight = noise(splits[1], (BANDS, SECTORS, NB, BC, P_SIZE), BC ** -0.5, 0.75, ((0, 4), (1, 8)))
    block_target = draw_block_target(jax.random.fold_in(splits[13], 71), 0)
    block_count = draw_block_count(jax.random.fold_in(splits[13], 71), 0)
    border_state = noise(splits[4], (BANDS, SECTORS, NS, C, BC), 1.0, 6.0, ((0, 4), (1, 8)))
    border_weight = noise(splits[5], (BANDS, SECTORS, NS, BC, P_SIZE), BC ** -0.5, 0.75, ((0, 4), (1, 8)))
    border_target = set_ends(jax.random.randint(splits[6], (BANDS, SECTORS, NS), 0, 2 * EP), jax.random.fold_in(splits[6], 1), 0, (2 * EP) - 1).astype(jnp.int32)
    kernel_one = noise(splits[7], (7, 7, C, C1), (49 * C) ** -0.5, 0.15625)
    bias_one = noise(splits[8], (C1,), 1.0, 4.0, (), jnp.float32)
    gain_one = jnp.clip(1.0 + 0.18 * jax.random.normal(splits[9], (C1,), jnp.float32), 0.1, 1.9)
    kernel_two = noise(splits[10], (7, 7, C1, C2), (49 * C1) ** -0.5, 0.109375)
    bias_two = noise(splits[11], (C2,), 1.0, 4.0, (), jnp.float32)
    gain_two = jnp.clip(1.0 + 0.18 * jax.random.normal(splits[12], (C2,), jnp.float32), 0.1, 1.9)
    return dict(cell_state=cell_state, remap_weight=remap_weight, block_target=block_target, block_count=block_count, border_state=border_state, border_weight=border_weight, border_target=border_target, kernel_one=kernel_one, bias_one=bias_one, gain_one=gain_one, kernel_two=kernel_two, bias_two=bias_two, gain_two=gain_two)


def to_image(totals, row_count, col_count):
    channels = totals.shape[1]
    shaped = totals.reshape(row_count, col_count, channels, PH, PW)
    return shaped.transpose(2, 0, 3, 1, 4).reshape(channels, row_count * PH, col_count * PW)

def block_sums(states, weights, slot_index, segments):
    products = jnp.einsum('ncb,nbp->ncp', states.astype(jnp.float32), weights.astype(jnp.float32), precision=lax.Precision.HIGHEST)
    return jax.ops.segment_sum(products, slot_index, num_segments=segments + 1)[:segments]

def pole_pad(raster):
    half_turn = raster.shape[2] // 2
    upper = jnp.roll(raster[:, :3][:, ::-1], half_turn, axis=2)
    bottom = jnp.roll(raster[:, -3:][:, ::-1], half_turn, axis=2)
    heightened = jnp.concatenate([upper, raster, bottom], 1)
    return jnp.concatenate([heightened[:, :, -3:], heightened, heightened[:, :, :3]], 2)

def conv_layer(raster, kernel, bias_term, gain_term, band_rows, channels_last):
    padded = pole_pad(raster)
    layout = ('NCHW', 'HWIO', 'NHWC') if channels_last else ('NCHW', 'HWIO', 'NCHW')
    results = []
    for band_no in range(BANDS):
        band_piece = padded[:, band_no * band_rows:band_no * band_rows + band_rows + 6].astype(jnp.float32)[None]
        conv_out = lax.conv_general_dilated(band_piece, kernel.astype(jnp.float32), (2, 2), 'VALID', dimension_numbers=layout, precision=lax.Precision.HIGHEST)[0]
        if channels_last:
            conv_out = conv_out + bias_term
            scaled = conv_out * lax.rsqrt(lax.optimization_barrier(jnp.mean(conv_out * conv_out, axis=-1, keepdims=True)) + 1e-05) * gain_term
        else:
            conv_out = conv_out + bias_term[:, None, None]
            scaled = conv_out * lax.rsqrt(lax.optimization_barrier(jnp.mean(conv_out * conv_out, axis=0, keepdims=True)) + 1e-05) * gain_term[:, None, None]
        results.append(jax.nn.gelu(scaled, approximate=True).astype(jnp.bfloat16))
    return jnp.concatenate(results, 0 if channels_last else 1)

def reference(cell_state, remap_weight, block_target, block_count, border_state, border_weight, border_target, kernel_one, bias_one, gain_one, kernel_two, bias_two, gain_two):
    slot_numbers = jnp.arange(NB, dtype=jnp.int32)

    def tile_field(device_flat):
        band_no = device_flat // SECTORS
        sector = device_flat % SECTORS
        west_sector = (sector + SECTORS - 1) % SECTORS
        east_sector = (sector + 1) % SECTORS
        slot_index = jnp.where(slot_numbers < block_count[band_no, sector], block_target[band_no, sector], NP).astype(jnp.int32)
        inner = block_sums(cell_state[band_no, sector], remap_weight[band_no, sector], slot_index, NP)
        from_west = block_sums(border_state[band_no, west_sector], border_weight[band_no, west_sector], border_target[band_no, west_sector], 2 * EP)[EP:]
        from_east = block_sums(border_state[band_no, east_sector], border_weight[band_no, east_sector], border_target[band_no, east_sector], 2 * EP)[:EP]
        raster = to_image(inner, PR, PC)
        raster = raster.at[:, :, :EDGE * PW].add(to_image(from_west, PR, EDGE))
        raster = raster.at[:, :, W - EDGE * PW:].add(to_image(from_east, PR, EDGE))
        return raster.astype(jnp.bfloat16)
    tiles = lax.map(tile_field, jnp.arange(BANDS * SECTORS, dtype=jnp.int32))
    field = tiles.reshape(BANDS, SECTORS, C, TH, W).transpose(2, 0, 3, 1, 4).reshape(C, ROWS, COLS)
    hidden = conv_layer(field, kernel_one, bias_one, gain_one, TH, False)
    return conv_layer(hidden, kernel_two, bias_two, gain_two, TH // 2, True)
```

```python
import functools

import jax
import jax.numpy as jnp
import numpy as np
from jax import lax
from jax.experimental import pallas as pl
from jax.experimental.pallas import tpu as pltpu
from jax.sharding import PartitionSpec as P

PH = 8
PW = 16
EDGE = 1
TH = 256
W = 128
PACK = 4
VMEM_LIMIT = 56 * 1024 * 1024
F32 = jnp.float32
BF16 = jnp.bfloat16


def params():
    return pltpu.CompilerParams(vmem_limit_bytes=VMEM_LIMIT)


def packed_states(states):
    n, c, b = states.shape
    return states.reshape(n // PACK, PACK, c, b).transpose(0, 2, 1, 3).reshape(n // PACK, c, PACK * b)


def group_product(s_ref, w_ref, mask, g, channels):
    s = s_ref[g]
    rows = w_ref.shape[1] * PACK
    lhs = jnp.concatenate([s] * PACK, axis=0) * mask
    rhs = w_ref[pl.ds(g * PACK, PACK)].reshape(rows, w_ref.shape[2])
    return jnp.dot(lhs, rhs, preferred_element_type=F32)


def slot_mask(channels, cells):
    row = lax.broadcasted_iota(jnp.int32, (PACK * channels, PACK * cells), 0) // channels
    col = lax.broadcasted_iota(jnp.int32, (PACK * channels, PACK * cells), 1) // cells
    return jnp.where(row == col, 1.0, 0.0).astype(BF16)


def border_kernel(target_ref, s_ref, w_ref, out_ref, acc):
    step = pl.program_id(0)
    channels = s_ref.shape[1]
    groups = s_ref.shape[0]

    @pl.when(step == 0)
    def _():
        acc[...] = jnp.zeros_like(acc)

    mask = slot_mask(channels, w_ref.shape[1])

    def body(i, _):
        for u in range(4):
            g = i * 4 + u
            prod = group_product(s_ref, w_ref, mask, g, channels)
            for k in range(PACK):
                t = target_ref[(step * groups + g) * PACK + k]
                acc[t] += prod[k * channels : (k + 1) * channels]
        return 0

    lax.fori_loop(0, groups // 4, body, 0)

    @pl.when(step == pl.num_programs(0) - 1)
    def _():
        out_ref[...] = acc[...].astype(BF16)


def border_sums(states, weights, targets, count):
    n, c, b = states.shape
    pixels = weights.shape[2]
    block = 64
    return pl.pallas_call(
        border_kernel,
        grid_spec=pltpu.PrefetchScalarGridSpec(
            num_scalar_prefetch=1,
            grid=(n // block,),
            in_specs=[
                pl.BlockSpec((block // PACK, c, PACK * b), lambda i, t: (i, 0, 0)),
                pl.BlockSpec((block, b, pixels), lambda i, t: (i, 0, 0)),
            ],
            out_specs=pl.BlockSpec((count, c, pixels), lambda i, t: (0, 0, 0)),
            scratch_shapes=[pltpu.VMEM((count, c, pixels), F32)],
        ),
        out_shape=jax.ShapeDtypeStruct((count, c, pixels), BF16),
        compiler_params=params(),
        name="border_sums",
    )(targets, packed_states(states), weights)


def inner_kernel(first_steps, target_ref, live_ref, s_ref, w_ref, acc):
    step = pl.program_id(0)
    channels = s_ref.shape[1]
    groups = s_ref.shape[0]
    mask = slot_mask(channels, w_ref.shape[1])

    def run(store):
        def body(i, _):
            for u in range(4):
                g = i * 4 + u
                prod = group_product(s_ref, w_ref, mask, g, channels)
                for k in range(PACK):
                    store((step * groups + g) * PACK + k, prod[k * channels : (k + 1) * channels])
            return 0

        lax.fori_loop(0, groups // 4, body, 0)

    @pl.when(step < first_steps)
    def _():
        def put(slot, value):
            acc[target_ref[slot]] = value

        run(put)

    @pl.when((step >= first_steps) & (step * groups * PACK < live_ref[0]))
    def _():
        def add(slot, value):
            alive = jnp.where(slot < live_ref[0], 1.0, 0.0)
            acc[target_ref[slot]] += value * alive

        run(add)


def inner_sums(states, weights, targets, live, patches):
    n, c, b = states.shape
    pixels = weights.shape[2]
    block = 64
    return pl.pallas_call(
        functools.partial(inner_kernel, patches // block),
        grid_spec=pltpu.PrefetchScalarGridSpec(
            num_scalar_prefetch=2,
            grid=(n // block,),
            in_specs=[
                pl.BlockSpec((block // PACK, c, PACK * b), lambda i, t, l: (i, 0, 0)),
                pl.BlockSpec((block, b, pixels), lambda i, t, l: (i, 0, 0)),
            ],
            out_specs=pl.BlockSpec((patches, c, pixels), lambda i, t, l: (0, 0, 0)),
        ),
        out_shape=jax.ShapeDtypeStruct((patches, c, pixels), F32),
        compiler_params=params(),
        name="inner_sums",
    )(targets, live, packed_states(states), weights)


def placement():
    j, ph, pw = np.meshgrid(np.arange(PACK), np.arange(PH), np.arange(PW), indexing="ij")
    f = (ph % 2) * 2 + pw % 2
    positions = PACK * PH * PW // 4
    rx2 = (pw // 2) % 2
    pos = ((rx2 * (PH // 2) + ph // 2) * PACK + j) * (PW // 4) + pw // 4
    table = np.zeros((PACK * PH * PW, 4 * positions), np.float32)
    table[np.arange(table.shape[0]), (f * positions + pos).ravel()] = 1.0
    return table


def field_kernel(cols, acc_ref, west_ref, east_ref, place_ref, out_ref):
    prows = out_ref.shape[0] // (PH // 4)
    channels = acc_ref.shape[1]
    wide = PACK * (PW // 4)
    rows = []
    for r in range(prows):
        for jg in range(cols // PACK):
            parts = []
            for j in range(PACK):
                col = jg * PACK + j
                v = acc_ref[r * cols + col]
                if col == 0:
                    v = v + west_ref[r].astype(F32)
                if col == cols - 1:
                    v = v + east_ref[r].astype(F32)
                parts.append(v.astype(BF16))
            rows.append(jnp.concatenate(parts, axis=1))
    moved = jnp.dot(jnp.concatenate(rows, axis=0), place_ref[...], preferred_element_type=F32)
    npos = moved.shape[1] // 4
    at = 0
    for r in range(prows):
        for jg in range(cols // PACK):
            part = moved[at : at + channels]
            at += channels
            stacked = jnp.concatenate([part[:, f * npos : (f + 1) * npos] for f in range(4)], axis=0)
            turned = stacked.T.astype(BF16)
            for rx2 in range(2):
                for py in range(PH // 2):
                    start = (rx2 * (PH // 2) + py) * wide
                    lane = ((py % 2) * 2 + rx2) * 4 * channels
                    out_ref[
                        r * (PH // 4) + py // 2, jg * wide : (jg + 1) * wide, lane : lane + 4 * channels
                    ] = turned[start : start + wide]


def build_field(acc, west, east, patch_rows, patch_cols):
    _, c, pixels = acc.shape
    step = 4
    per = step * PH // 4
    place = jnp.asarray(placement(), BF16)
    return pl.pallas_call(
        functools.partial(field_kernel, patch_cols),
        grid=(patch_rows // step,),
        in_specs=[
            pl.BlockSpec((step * patch_cols, c, pixels), lambda i: (i, 0, 0)),
            pl.BlockSpec((step, c, pixels), lambda i: (i, 0, 0)),
            pl.BlockSpec((step, c, pixels), lambda i: (i, 0, 0)),
            pl.BlockSpec(place.shape, lambda i: (0, 0)),
        ],
        out_specs=pl.BlockSpec((per, patch_cols * PW // 4, 16 * c), lambda i: (i, 0, 0)),
        out_shape=jax.ShapeDtypeStruct((patch_rows * PH // 4, patch_cols * PW // 4, 16 * c), BF16),
        compiler_params=params(),
        name="field",
    )(acc, west, east, place)


def halo(x, above, below, left, right, flip):
    nlat, nlon = lax.axis_size("lat"), lax.axis_size("lon")
    rows, cols, _ = x.shape
    west = lax.ppermute(x[:, cols - left :], "lon", [(i, (i + 1) % nlon) for i in range(nlon)])
    east = lax.ppermute(x[:, :right], "lon", [((i + 1) % nlon, i) for i in range(nlon)])

    def wide(a, b):
        return jnp.concatenate([west[a:b], x[a:b], east[a:b]], axis=1)

    lat = lax.axis_index("lat")
    is_top, is_bottom = lat == 0, lat == nlat - 1
    top, bottom = wide(0, above), wide(rows - above, rows)
    down = lax.ppermute(bottom, "lat", [(i, i + 1) for i in range(nlat - 1)])
    up = lax.ppermute(top[:below], "lat", [(i + 1, i) for i in range(nlat - 1)])
    pole = jnp.where(is_top, flip(top), flip(bottom))
    pole = lax.ppermute(pole, "lon", [((i + nlon // 2) % nlon, i) for i in range(nlon)])
    north = jnp.where(is_top, pole, down)
    south = jnp.where(is_bottom, pole[:below], up)

    def side(a, b, middle):
        return jnp.concatenate([north[:, a:b], middle, south[:, a:b]], axis=0).astype(F32)

    return (
        north[:, left : left + cols],
        south[:, left : left + cols],
        side(0, left, west),
        side(left + cols, left + cols + right, east),
    )


def fill_shifted(xs, x_ref, north_ref, south_ref, west_ref, east_ref, left, right):
    rows, cols, _ = x_ref.shape
    above, below = north_ref.shape[0], south_ref.shape[0]

    def put(y, line):
        xs[left, y] = line
        wide = line.astype(F32)
        spot = lax.broadcasted_iota(jnp.int32, wide.shape, 0)
        for k in range(1, left + 1):
            moved = pltpu.roll(wide, k, 0)
            for i in range(k):
                moved = jnp.where(spot == i, west_ref[y, pl.ds(left - k + i, 1)], moved)
            xs[left - k, y] = moved.astype(BF16)
        for k in range(1, right + 1):
            moved = pltpu.roll(wide, cols - k, 0)
            for i in range(k):
                moved = jnp.where(spot == cols - k + i, east_ref[y, pl.ds(i, 1)], moved)
            xs[left + k, y] = moved.astype(BF16)

    for y in range(above):
        put(y, north_ref[y])

    def body(i, _):
        for u in range(2):
            y = i * 2 + u
            put(above + y, x_ref[y])
        return 0

    lax.fori_loop(0, rows // 2, body, 0)
    for y in range(below):
        put(above + rows + y, south_ref[y])


def gelu(v):
    inner = np.float32(np.sqrt(2 / np.pi)) * (v + np.float32(0.044715) * (v * v * v))
    return 0.5 * v * (1.0 + jnp.tanh(inner))


def conv_kernel(
    left, right, groups, x_ref, north_ref, south_ref, west_ref, east_ref, w_ref, bias_ref, gain_ref, out_ref, xs
):
    rows, cols, channels = x_ref.shape
    outs = w_ref.shape[2]
    fill_shifted(xs, x_ref, north_ref, south_ref, west_ref, east_ref, left, right)
    taps_y = north_ref.shape[0] + south_ref.shape[0] + 1
    taps_x = left + right + 1
    chunk = 8
    size = outs // groups
    if groups > 1:
        row = lax.broadcasted_iota(jnp.int32, (outs, outs), 0) // size
        col = lax.broadcasted_iota(jnp.int32, (outs, outs), 1) // size
        average = jnp.where(row == col, 1.0 / size, 0.0).astype(BF16)
    bias, gain = bias_ref[...], gain_ref[...]

    def body(i, _):
        y0 = i * chunk
        total = jnp.zeros((chunk * cols, outs), F32)
        for dy in range(taps_y):
            for dx in range(taps_x):
                lhs = xs[dx, pl.ds(y0 + dy, chunk)].reshape(chunk * cols, channels)
                total += jnp.dot(lhs, w_ref[dy * taps_x + dx], preferred_element_type=F32)
        total += bias
        square = total * total
        if groups > 1:
            high = square.astype(BF16)
            low = (square - high.astype(F32)).astype(BF16)
            mean = jnp.dot(high, average, preferred_element_type=F32) + jnp.dot(
                low, average, preferred_element_type=F32
            )
        else:
            mean = jnp.mean(square, axis=-1, keepdims=True)
        scaled = total * lax.rsqrt(mean + 1e-5) * gain
        out_ref[pl.ds(y0, chunk)] = gelu(scaled).astype(BF16).reshape(chunk, cols, outs)
        return 0

    lax.fori_loop(0, rows // chunk, body, 0)


def conv_block(x, edges, weights, bias, gain, left, right, groups, name):
    rows, cols, channels = x.shape
    north, south, west, east = edges
    outs = weights.shape[2]
    vmem = pl.BlockSpec(memory_space=pltpu.VMEM)
    return pl.pallas_call(
        functools.partial(conv_kernel, left, right, groups),
        in_specs=[vmem] * 8,
        out_specs=vmem,
        out_shape=jax.ShapeDtypeStruct((rows, cols, outs), BF16),
        scratch_shapes=[pltpu.VMEM((left + right + 1, rows + north.shape[0] + south.shape[0], cols, channels), BF16)],
        compiler_params=params(),
        name=name,
    )(x, north, south, west, east, weights, jnp.tile(bias, groups)[None], jnp.tile(gain, groups)[None])


def weights_one(kernel):
    _, _, ci, co = kernel.shape
    parts = []
    for sy in range(2):
        for sx in range(2):
            parts.append(jnp.pad(kernel, ((1 + 2 * sy, 4 - 2 * sy), (1 + 2 * sx, 4 - 2 * sx), (0, 0), (0, 0))))
    full = jnp.concatenate(parts, axis=-1)
    full = full.reshape(3, 2, 2, 3, 2, 2, ci, 4 * co).transpose(0, 3, 1, 4, 2, 5, 6, 7)
    return full.reshape(9, 16 * ci, 4 * co)


def weights_two(kernel):
    _, _, ci, co = kernel.shape
    full = jnp.pad(kernel, ((1, 0), (1, 0), (0, 0), (0, 0)))
    return full.reshape(4, 2, 4, 2, ci, co).transpose(0, 2, 1, 3, 4, 5).reshape(16, 4 * ci, co)


def flip_one(rows):
    n, cols, ch = rows.shape
    split = rows[::-1].reshape(n, cols, 2, 2, 2, ch // 8)
    return split[:, :, ::-1, :, ::-1].reshape(n, cols, ch)


def flip_two(rows):
    half = rows.shape[2] // 2
    return jnp.concatenate([rows[::-1, :, half:], rows[::-1, :, :half]], axis=2)


def local(
    cell_state,
    remap_weight,
    block_target,
    block_count,
    border_state,
    border_weight,
    border_target,
    kernel_one,
    bias_one,
    gain_one,
    kernel_two,
    bias_two,
    gain_two,
):
    patch_rows = TH // PH
    patch_cols = W // PW
    rim = EDGE * patch_rows
    nlon = lax.axis_size("lon")
    border = border_sums(border_state[0, 0], border_weight[0, 0], border_target[0, 0], 2 * rim)
    from_west = lax.ppermute(border[rim:], "lon", [(i, (i + 1) % nlon) for i in range(nlon)])
    from_east = lax.ppermute(border[:rim], "lon", [((i + 1) % nlon, i) for i in range(nlon)])
    acc = inner_sums(
        cell_state[0, 0], remap_weight[0, 0], block_target[0, 0], block_count[0], patch_rows * patch_cols
    )
    field = build_field(acc, from_west, from_east, patch_rows, patch_cols)
    one = weights_one(kernel_one)
    two = weights_two(kernel_two)
    hidden = conv_block(field, halo(field, 1, 1, 1, 1, flip_one), one, bias_one, gain_one, 1, 1, 4, "first")
    return conv_block(hidden, halo(hidden, 2, 1, 2, 1, flip_two), two, bias_two, gain_two, 2, 1, 1, "second")


def solution(mesh):
    placed = (
        P("lat", "lon", None, None, None),
        P("lat", "lon", None, None, None),
        P("lat", "lon", None),
        P("lat", "lon"),
        P("lat", "lon", None, None, None),
        P("lat", "lon", None, None, None),
        P("lat", "lon", None),
        P(),
        P(),
        P(),
        P(),
        P(),
        P(),
    )
    return jax.shard_map(
        local, mesh=mesh, in_specs=placed, out_specs=P("lat", "lon", None), check_vma=False
    )
```

```python
import functools

import jax
import jax.numpy as jnp
import numpy as np
from jax import lax
from jax.experimental import pallas as pl
from jax.experimental.pallas import tpu as pltpu
from jax.sharding import PartitionSpec as P

PH = 8
PW = 16
EDGE = 1
TH = 256
W = 128
PACK = 4
VMEM_LIMIT = 56 * 1024 * 1024
F32 = jnp.float32
BF16 = jnp.bfloat16


def params():
    return pltpu.CompilerParams(vmem_limit_bytes=VMEM_LIMIT)


def turn_states(s_ref, turned, distance):
    channels, _, block = s_ref.shape

    def body(i, _):
        for u in range(2):
            c = i * 2 + u
            v = s_ref[c].astype(F32)
            if block == distance * 2 and distance % 128 == 0:
                pair = jnp.concatenate([v[:, :distance], v[:, distance:]], axis=0)
            else:
                pair = jnp.concatenate([v, pltpu.roll(v, block - distance, 1)], axis=0)
            pair = pair.T
            turned[pl.ds(c, pair.shape[0], stride=channels)] = pair
        return 0

    lax.fori_loop(0, channels // 2, body, 0)


def group_slots(g, distance):
    return (2 * g, 2 * g + distance, 2 * g + 1, 2 * g + 1 + distance)


def group_product(turned, w_ref, mask, g, channels, distance):
    start = pl.multiple_of(g * 2 * channels, 2 * channels)
    s = jnp.concatenate(
        [turned[pl.ds(start, channels)], turned[pl.ds(start + channels, channels)]], axis=1
    ).astype(BF16)
    lhs = jnp.concatenate([s] * PACK, axis=0) * mask
    rhs = jnp.concatenate([w_ref[slot] for slot in group_slots(g, distance)], axis=0)
    return jnp.dot(lhs, rhs, preferred_element_type=F32)


def slot_mask(channels, cells):
    row = lax.broadcasted_iota(jnp.int32, (PACK * channels, PACK * cells), 0) // channels
    col = lax.broadcasted_iota(jnp.int32, (PACK * channels, PACK * cells), 1) // cells
    return jnp.where(row == col, 1.0, 0.0).astype(BF16)


def add_groups(base, s_ref, w_ref, turned, store):
    channels, cells, block = s_ref.shape
    distance = block // 2
    turn_states(s_ref, turned, distance)
    mask = slot_mask(channels, cells)

    def body(i, _):
        for u in range(4):
            g = i * 4 + u
            prod = group_product(turned, w_ref, mask, g, channels, distance)
            for k, slot in enumerate(group_slots(g, distance)):
                store(base + slot, prod[k * channels : (k + 1) * channels])
        return 0

    lax.fori_loop(0, block // (4 * PACK), body, 0)


def border_kernel(target_ref, s_ref, w_ref, out_ref, acc, turned):
    acc[...] = jnp.zeros_like(acc)

    def add(slot, value):
        acc[target_ref[slot]] += value

    add_groups(0, s_ref, w_ref, turned, add)
    out_ref[...] = acc[...].astype(BF16)


def border_sums(states, weights, targets, count):
    n, c, b = states.shape
    pixels = weights.shape[2]
    return pl.pallas_call(
        border_kernel,
        grid_spec=pltpu.PrefetchScalarGridSpec(
            num_scalar_prefetch=1,
            grid=(1,),
            in_specs=[
                pl.BlockSpec((c, b, n), lambda i, t: (0, 0, 0)),
                pl.BlockSpec((n, b, pixels), lambda i, t: (0, 0, 0)),
            ],
            out_specs=pl.BlockSpec((count, c, pixels), lambda i, t: (0, 0, 0)),
            scratch_shapes=[pltpu.VMEM((count, c, pixels), F32), pltpu.VMEM((n * c, 2 * b), F32)],
        ),
        out_shape=jax.ShapeDtypeStruct((count, c, pixels), BF16),
        compiler_params=params(),
        name="border_sums",
    )(targets, states.transpose(1, 2, 0), weights)


def inner_kernel(first_steps, target_ref, live_ref, s_ref, w_ref, acc, turned):
    step = pl.program_id(0)
    base = step * s_ref.shape[2]

    @pl.when(step < first_steps)
    def _():
        def put(slot, value):
            acc[target_ref[slot]] = value

        add_groups(base, s_ref, w_ref, turned, put)

    @pl.when((step >= first_steps) & (base < live_ref[0]))
    def _():
        def add(slot, value):
            alive = jnp.where(slot < live_ref[0], 1.0, 0.0)
            acc[target_ref[slot]] += value * alive

        add_groups(base, s_ref, w_ref, turned, add)


def inner_sums(states, weights, targets, live, patches):
    n, c, b = states.shape
    pixels = weights.shape[2]
    block = patches
    return pl.pallas_call(
        functools.partial(inner_kernel, patches // block),
        grid_spec=pltpu.PrefetchScalarGridSpec(
            num_scalar_prefetch=2,
            grid=(n // block,),
            in_specs=[
                pl.BlockSpec((c, b, block), lambda i, t, l: (0, 0, i)),
                pl.BlockSpec((block, b, pixels), lambda i, t, l: (i, 0, 0)),
            ],
            out_specs=pl.BlockSpec((patches, c, pixels), lambda i, t, l: (0, 0, 0)),
            scratch_shapes=[pltpu.VMEM((block // 2 * c, 2 * b), F32)],
        ),
        out_shape=jax.ShapeDtypeStruct((patches, c, pixels), F32),
        compiler_params=params(),
        name="inner_sums",
    )(targets, live, states.transpose(1, 2, 0), weights)


def placement():
    j, ph, pw = np.meshgrid(np.arange(PACK), np.arange(PH), np.arange(PW), indexing="ij")
    f = (ph % 2) * 2 + pw % 2
    positions = PACK * PH * PW // 4
    rx2 = (pw // 2) % 2
    pos = ((rx2 * (PH // 2) + ph // 2) * PACK + j) * (PW // 4) + pw // 4
    table = np.zeros((PACK * PH * PW, 4 * positions), np.float32)
    table[np.arange(table.shape[0]), (f * positions + pos).ravel()] = 1.0
    return table


def field_kernel(cols, acc_ref, west_ref, east_ref, place_ref, out_ref):
    prows = out_ref.shape[0] // (PH // 4)
    channels = acc_ref.shape[1]
    wide = PACK * (PW // 4)
    rows = []
    for r in range(prows):
        for jg in range(cols // PACK):
            parts = []
            for j in range(PACK):
                col = jg * PACK + j
                v = acc_ref[r * cols + col]
                if col == 0:
                    v = v + west_ref[r].astype(F32)
                if col == cols - 1:
                    v = v + east_ref[r].astype(F32)
                parts.append(v.astype(BF16))
            rows.append(jnp.concatenate(parts, axis=1))
    moved = jnp.dot(jnp.concatenate(rows, axis=0), place_ref[...], preferred_element_type=F32)
    npos = moved.shape[1] // 4
    at = 0
    for r in range(prows):
        for jg in range(cols // PACK):
            part = moved[at : at + channels]
            at += channels
            stacked = jnp.concatenate([part[:, f * npos : (f + 1) * npos] for f in range(4)], axis=0)
            turned = stacked.T.astype(BF16)
            for rx2 in range(2):
                for py in range(PH // 2):
                    start = (rx2 * (PH // 2) + py) * wide
                    lane = ((py % 2) * 2 + rx2) * 4 * channels
                    out_ref[
                        r * (PH // 4) + py // 2, jg * wide : (jg + 1) * wide, lane : lane + 4 * channels
                    ] = turned[start : start + wide]


def build_field(acc, west, east, patch_rows, patch_cols):
    _, c, pixels = acc.shape
    step = 4
    per = step * PH // 4
    place = jnp.asarray(placement(), BF16)
    return pl.pallas_call(
        functools.partial(field_kernel, patch_cols),
        grid=(patch_rows // step,),
        in_specs=[
            pl.BlockSpec((step * patch_cols, c, pixels), lambda i: (i, 0, 0)),
            pl.BlockSpec((step, c, pixels), lambda i: (i, 0, 0)),
            pl.BlockSpec((step, c, pixels), lambda i: (i, 0, 0)),
            pl.BlockSpec(place.shape, lambda i: (0, 0)),
        ],
        out_specs=pl.BlockSpec((per, patch_cols * PW // 4, 16 * c), lambda i: (i, 0, 0)),
        out_shape=jax.ShapeDtypeStruct((patch_rows * PH // 4, patch_cols * PW // 4, 16 * c), BF16),
        compiler_params=params(),
        name="field",
    )(acc, west, east, place)


def flip_lines(v, swap):
    pieces = [v[:, i : i + 128] for i in range(0, v.shape[1], 128)]
    half = len(pieces) // 2
    pieces = pieces[half:] + pieces[:half]
    if swap:
        pieces = [pltpu.roll(p, swap, 1) for p in pieces]
    return jnp.concatenate(pieces, axis=1)


def exchange_kernel(
    nlat, nlon, left, right, below, swap,
    x_ref, north_ref, south_ref, west_ref, east_ref,
    col_e, col_w, send_e, send_w, recv_w, recv_e, lines, corner_w, corner_e, send_sem, recv_sem,
):
    rows, cols, _ = x_ref.shape
    above = lines.shape[1]
    tile = corner_w.shape[2]
    lat, lon = lax.axis_index("lat"), lax.axis_index("lon")
    is_top, is_bottom = (nlat - lat) // nlat, (lat + 1) // nlat
    west = (lat, (lon + nlon - 1) % nlon)
    east = (lat, (lon + 1) % nlon)

    def up(d):
        return (lat - 1 + is_top, (lon + is_top * (nlon // 2) + d + nlon) % nlon)

    def down(d):
        return (lat + 1 - is_bottom, (lon + is_bottom * (nlon // 2) + d + nlon) % nlon)

    barrier = pltpu.get_barrier_semaphore()
    partners = [west, east] + [up(d) for d in (-1, 0, 1)] + [down(d) for d in (-1, 0, 1)]
    for partner in partners:
        pl.semaphore_signal(barrier, inc=1, device_id=partner, device_id_type=pl.DeviceIdType.MESH)

    def body(y, _):
        v = x_ref[y].astype(F32)
        for i in range(left):
            col_e[i, pl.ds(y, 1)] = v[cols - left + i : cols - left + i + 1]
        for i in range(right):
            col_w[i, pl.ds(y, 1)] = v[i : i + 1]
        return 0

    lax.fori_loop(0, rows, body, 0)
    send_e[...] = col_e[...].astype(BF16)
    send_w[...] = col_w[...].astype(BF16)
    pl.semaphore_wait(barrier, len(partners))

    copies = []

    def send(src, dst, slot, device):
        copy = pltpu.make_async_remote_copy(
            src_ref=src,
            dst_ref=dst,
            send_sem=send_sem.at[len(copies)],
            recv_sem=recv_sem.at[slot],
            device_id=device,
            device_id_type=pl.DeviceIdType.MESH,
        )
        copy.start()
        copies.append(copy)

    send(send_e, recv_w, 0, east)
    send(send_w, recv_e, 1, west)
    for place, y0, side in ((up, 0, 1 - is_top), (down, rows - above, is_bottom)):
        send(x_ref.at[pl.ds(y0, above)], lines.at[side], 2 + side * 3, place(0))
        send(x_ref.at[pl.ds(y0, above), pl.ds(cols - tile, tile)], corner_w.at[side], 3 + side * 3, place(1))
        send(x_ref.at[pl.ds(y0, above), pl.ds(0, tile)], corner_e.at[side], 4 + side * 3, place(-1))
    for copy in copies:
        copy.wait_send()
    for slot, buffer in ((0, recv_w), (1, recv_e)):
        pltpu.make_async_copy(buffer, buffer, recv_sem.at[slot]).wait()
    for side in range(2):
        for k, buffer in enumerate((lines, corner_w, corner_e)):
            pltpu.make_async_copy(buffer.at[side], buffer.at[side], recv_sem.at[2 + side * 3 + k]).wait()

    def line(buffer, side, k):
        polar = is_top if side == 0 else is_bottom
        plain = buffer[side, k].astype(F32)
        mirrored = flip_lines(buffer[side, above - 1 - k].astype(F32), swap)
        share = jnp.where(polar == 1, 1.0, 0.0)
        return mirrored * share + plain * (1.0 - share)

    for i in range(left):
        west_ref[i, pl.ds(0, rows)] = recv_w[i].astype(F32)
    for i in range(right):
        east_ref[i, pl.ds(0, rows)] = recv_e[i].astype(F32)
    at = rows
    for side, count, ref in ((0, above, north_ref), (1, below, south_ref)):
        for k in range(count):
            ref[k] = line(lines, side, k).astype(BF16)
            corner = line(corner_w, side, k)
            for i in range(left):
                west_ref[i, pl.ds(at, 1)] = corner[tile - left + i : tile - left + i + 1]
            corner = line(corner_e, side, k)
            for i in range(right):
                east_ref[i, pl.ds(at, 1)] = corner[i : i + 1]
            at += 1


def halo(x, above, below, left, right, swap, collective_id):
    rows, cols, ch = x.shape
    tile = 16
    extra = rows + 8
    vmem = pl.BlockSpec(memory_space=pltpu.VMEM)
    return pl.pallas_call(
        functools.partial(
            exchange_kernel, lax.axis_size("lat"), lax.axis_size("lon"), left, right, below, swap
        ),
        in_specs=[vmem],
        out_specs=[vmem] * 4,
        out_shape=[
            jax.ShapeDtypeStruct((above, cols, ch), BF16),
            jax.ShapeDtypeStruct((below, cols, ch), BF16),
            jax.ShapeDtypeStruct((left, extra, ch), F32),
            jax.ShapeDtypeStruct((right, extra, ch), F32),
        ],
        scratch_shapes=[
            pltpu.VMEM((left, rows, ch), F32),
            pltpu.VMEM((right, rows, ch), F32),
            pltpu.VMEM((left, rows, ch), BF16),
            pltpu.VMEM((right, rows, ch), BF16),
            pltpu.VMEM((left, rows, ch), BF16),
            pltpu.VMEM((right, rows, ch), BF16),
            pltpu.VMEM((2, above, cols, ch), BF16),
            pltpu.VMEM((2, above, tile, ch), BF16),
            pltpu.VMEM((2, above, tile, ch), BF16),
            pltpu.SemaphoreType.DMA((8,)),
            pltpu.SemaphoreType.DMA((8,)),
        ],
        compiler_params=pltpu.CompilerParams(
            collective_id=collective_id, has_side_effects=True, vmem_limit_bytes=VMEM_LIMIT
        ),
        name="halo",
    )(x)


def fill_shifted(xs, x_ref, north_ref, south_ref, west_ref, east_ref, left, right):
    rows, cols, _ = x_ref.shape
    above, below = north_ref.shape[0], south_ref.shape[0]

    def put(y, line, edge):
        xs[left, y] = line
        wide = line.astype(F32)
        spot = lax.broadcasted_iota(jnp.int32, wide.shape, 0)
        for k in range(1, left + 1):
            moved = pltpu.roll(wide, k, 0)
            for i in range(k):
                moved = jnp.where(spot == i, west_ref[left - k + i, pl.ds(edge, 1)], moved)
            xs[left - k, y] = moved.astype(BF16)
        for k in range(1, right + 1):
            moved = pltpu.roll(wide, cols - k, 0)
            for i in range(k):
                moved = jnp.where(spot == cols - k + i, east_ref[i, pl.ds(edge, 1)], moved)
            xs[left + k, y] = moved.astype(BF16)

    for y in range(above):
        put(y, north_ref[y], rows + y)

    def body(i, _):
        for u in range(2):
            y = i * 2 + u
            put(above + y, x_ref[y], y)
        return 0

    lax.fori_loop(0, rows // 2, body, 0)
    for y in range(below):
        put(above + rows + y, south_ref[y], rows + above + y)


def gelu(v):
    inner = np.float32(np.sqrt(2 / np.pi)) * (v + np.float32(0.044715) * (v * v * v))
    return 0.5 * v * (1.0 + jnp.tanh(inner))


def conv_kernel(
    left, right, groups, x_ref, north_ref, south_ref, west_ref, east_ref, w_ref, bias_ref, gain_ref, out_ref, xs
):
    rows, cols, channels = x_ref.shape
    outs = w_ref.shape[2]
    fill_shifted(xs, x_ref, north_ref, south_ref, west_ref, east_ref, left, right)
    taps_y = north_ref.shape[0] + south_ref.shape[0] + 1
    taps_x = left + right + 1
    chunk = 8
    size = outs // groups
    if groups > 1:
        row = lax.broadcasted_iota(jnp.int32, (outs, outs), 0) // size
        col = lax.broadcasted_iota(jnp.int32, (outs, outs), 1) // size
        average = jnp.where(row == col, 1.0 / size, 0.0).astype(BF16)
    bias, gain = bias_ref[...], gain_ref[...]

    def body(i, _):
        y0 = i * chunk
        total = jnp.zeros((chunk * cols, outs), F32)
        for dy in range(taps_y):
            for dx in range(taps_x):
                lhs = xs[dx, pl.ds(y0 + dy, chunk)].reshape(chunk * cols, channels)
                total += jnp.dot(lhs, w_ref[dy * taps_x + dx], preferred_element_type=F32)
        total += bias
        square = total * total
        if groups > 1:
            high = square.astype(BF16)
            low = (square - high.astype(F32)).astype(BF16)
            mean = jnp.dot(high, average, preferred_element_type=F32) + jnp.dot(
                low, average, preferred_element_type=F32
            )
        else:
            mean = jnp.mean(square, axis=-1, keepdims=True)
        scaled = total * lax.rsqrt(mean + 1e-5) * gain
        out_ref[pl.ds(y0, chunk)] = gelu(scaled).astype(BF16).reshape(chunk, cols, outs)
        return 0

    lax.fori_loop(0, rows // chunk, body, 0)


def conv_block(x, edges, weights, bias, gain, left, right, groups, name):
    rows, cols, channels = x.shape
    north, south, west, east = edges
    outs = weights.shape[2]
    vmem = pl.BlockSpec(memory_space=pltpu.VMEM)
    return pl.pallas_call(
        functools.partial(conv_kernel, left, right, groups),
        in_specs=[vmem] * 8,
        out_specs=vmem,
        out_shape=jax.ShapeDtypeStruct((rows, cols, outs), BF16),
        scratch_shapes=[pltpu.VMEM((left + right + 1, rows + north.shape[0] + south.shape[0], cols, channels), BF16)],
        compiler_params=params(),
        name=name,
    )(x, north, south, west, east, weights, jnp.tile(bias, groups)[None], jnp.tile(gain, groups)[None])


def weights_one(kernel):
    _, _, ci, co = kernel.shape
    parts = []
    for sy in range(2):
        for sx in range(2):
            parts.append(jnp.pad(kernel, ((1 + 2 * sy, 4 - 2 * sy), (1 + 2 * sx, 4 - 2 * sx), (0, 0), (0, 0))))
    full = jnp.concatenate(parts, axis=-1)
    full = full.reshape(3, 2, 2, 3, 2, 2, ci, 4 * co).transpose(0, 3, 1, 4, 2, 5, 6, 7)
    return full.reshape(9, 16 * ci, 4 * co)


def weights_two(kernel):
    _, _, ci, co = kernel.shape
    full = jnp.pad(kernel, ((1, 0), (1, 0), (0, 0), (0, 0)))
    return full.reshape(4, 2, 4, 2, ci, co).transpose(0, 2, 1, 3, 4, 5).reshape(16, 4 * ci, co)


def local(
    cell_state,
    remap_weight,
    block_target,
    block_count,
    border_state,
    border_weight,
    border_target,
    kernel_one,
    bias_one,
    gain_one,
    kernel_two,
    bias_two,
    gain_two,
):
    patch_rows = TH // PH
    patch_cols = W // PW
    rim = EDGE * patch_rows
    nlon = lax.axis_size("lon")
    border = border_sums(border_state[0, 0], border_weight[0, 0], border_target[0, 0], 2 * rim)
    from_west = lax.ppermute(border[rim:], "lon", [(i, (i + 1) % nlon) for i in range(nlon)])
    from_east = lax.ppermute(border[:rim], "lon", [((i + 1) % nlon, i) for i in range(nlon)])
    acc = inner_sums(
        cell_state[0, 0], remap_weight[0, 0], block_target[0, 0], block_count[0], patch_rows * patch_cols
    )
    field = build_field(acc, from_west, from_east, patch_rows, patch_cols)
    one = weights_one(kernel_one)
    two = weights_two(kernel_two)
    hidden = conv_block(field, halo(field, 1, 1, 1, 1, 2 * kernel_one.shape[2], 0), one, bias_one, gain_one, 1, 1, 4, "first")
    return conv_block(hidden, halo(hidden, 2, 1, 2, 1, 0, 1), two, bias_two, gain_two, 2, 1, 1, "second")


def solution(mesh):
    placed = (
        P("lat", "lon", None, None, None),
        P("lat", "lon", None, None, None),
        P("lat", "lon", None),
        P("lat", "lon"),
        P("lat", "lon", None, None, None),
        P("lat", "lon", None, None, None),
        P("lat", "lon", None),
        P(),
        P(),
        P(),
        P(),
        P(),
        P(),
    )
    return jax.shard_map(
        local, mesh=mesh, in_specs=placed, out_specs=P("lat", "lon", None), check_vma=False
    )
```

```python
import functools

import jax
import jax.numpy as jnp
import numpy as np
from jax import lax
from jax.experimental import pallas as pl
from jax.experimental.pallas import tpu as pltpu
from jax.sharding import PartitionSpec as P

PH = 8
PW = 16
EDGE = 1
TH = 256
W = 128
PACK = 4
VMEM_LIMIT = 56 * 1024 * 1024
F32 = jnp.float32
BF16 = jnp.bfloat16


def params():
    return pltpu.CompilerParams(vmem_limit_bytes=VMEM_LIMIT)


def turn_states(s_ref, turned, distance):
    channels, _, block = s_ref.shape

    def body(i, _):
        for u in range(2):
            c = i * 2 + u
            v = s_ref[c]
            if block == distance * 2 and distance % 128 == 0:
                pair = jnp.concatenate([v[:, :distance], v[:, distance:]], axis=0)
            else:
                other = pltpu.roll(v.astype(F32), block - distance, 1).astype(BF16)
                pair = jnp.concatenate([v, other], axis=0)
            pair = pair.T.astype(F32)
            turned[pl.ds(c, pair.shape[0], stride=channels)] = pair
        return 0

    lax.fori_loop(0, channels // 2, body, 0)


def group_slots(g, distance):
    return (2 * g, 2 * g + distance, 2 * g + 1, 2 * g + 1 + distance)


def group_product(turned, w_ref, mask, g, channels, distance):
    start = pl.multiple_of(g * 2 * channels, 2 * channels)
    s = jnp.concatenate(
        [turned[pl.ds(start, channels)], turned[pl.ds(start + channels, channels)]], axis=1
    ).astype(BF16)
    lhs = jnp.concatenate([s] * PACK, axis=0) * mask
    rhs = jnp.concatenate([w_ref[slot] for slot in group_slots(g, distance)], axis=0)
    return jnp.dot(lhs, rhs, preferred_element_type=F32)


def slot_mask(channels, cells):
    row = lax.broadcasted_iota(jnp.int32, (PACK * channels, PACK * cells), 0) // channels
    col = lax.broadcasted_iota(jnp.int32, (PACK * channels, PACK * cells), 1) // cells
    return jnp.where(row == col, 1.0, 0.0).astype(BF16)


def add_groups(base, s_ref, w_ref, turned, store):
    channels, cells, block = s_ref.shape
    distance = block // 2
    turn_states(s_ref, turned, distance)
    mask = slot_mask(channels, cells)

    def body(i, _):
        for u in range(4):
            g = i * 4 + u
            prod = group_product(turned, w_ref, mask, g, channels, distance)
            for k, slot in enumerate(group_slots(g, distance)):
                store(base + slot, prod[k * channels : (k + 1) * channels])
        return 0

    lax.fori_loop(0, block // (4 * PACK), body, 0)


def border_kernel(target_ref, s_ref, w_ref, west_ref, east_ref, acc, turned):
    acc[...] = jnp.zeros_like(acc)

    def add(slot, value):
        acc[target_ref[slot]] += value

    add_groups(0, s_ref, w_ref, turned, add)
    half = west_ref.shape[0]
    west_ref[...] = acc[:half].astype(BF16)
    east_ref[...] = acc[half:].astype(BF16)


def border_sums(states, weights, targets, count):
    n, c, b = states.shape
    pixels = weights.shape[2]
    return pl.pallas_call(
        border_kernel,
        grid_spec=pltpu.PrefetchScalarGridSpec(
            num_scalar_prefetch=1,
            grid=(1,),
            in_specs=[
                pl.BlockSpec((c, b, n), lambda i, t: (0, 0, 0)),
                pl.BlockSpec((n, b, pixels), lambda i, t: (0, 0, 0)),
            ],
            out_specs=[pl.BlockSpec((count // 2, c, pixels), lambda i, t: (0, 0, 0))] * 2,
            scratch_shapes=[pltpu.VMEM((count, c, pixels), F32), pltpu.VMEM((n * c, 2 * b), F32)],
        ),
        out_shape=[jax.ShapeDtypeStruct((count // 2, c, pixels), BF16)] * 2,
        compiler_params=params(),
        name="border_sums",
    )(targets, states.transpose(1, 2, 0), weights)


def inner_kernel(first_steps, target_ref, live_ref, s_ref, w_ref, acc, turned):
    step = pl.program_id(0)
    base = step * s_ref.shape[2]

    @pl.when(step < first_steps)
    def _():
        def put(slot, value):
            acc[target_ref[slot]] = value

        add_groups(base, s_ref, w_ref, turned, put)

    @pl.when((step >= first_steps) & (base < live_ref[0]))
    def _():
        def add(slot, value):
            alive = jnp.where(slot < live_ref[0], 1.0, 0.0)
            acc[target_ref[slot]] += value * alive

        add_groups(base, s_ref, w_ref, turned, add)


def inner_sums(states, weights, targets, live, patches):
    n, c, b = states.shape
    pixels = weights.shape[2]
    block = patches
    return pl.pallas_call(
        functools.partial(inner_kernel, patches // block),
        grid_spec=pltpu.PrefetchScalarGridSpec(
            num_scalar_prefetch=2,
            grid=(n // block,),
            in_specs=[
                pl.BlockSpec((c, b, block), lambda i, t, l: (0, 0, i)),
                pl.BlockSpec((block, b, pixels), lambda i, t, l: (i, 0, 0)),
            ],
            out_specs=pl.BlockSpec((patches, c, pixels), lambda i, t, l: (0, 0, 0)),
            scratch_shapes=[pltpu.VMEM((block // 2 * c, 2 * b), F32)],
        ),
        out_shape=jax.ShapeDtypeStruct((patches, c, pixels), F32),
        compiler_params=params(),
        name="inner_sums",
    )(targets, live, states.transpose(1, 2, 0), weights)


def placement():
    j, ph, pw = np.meshgrid(np.arange(PACK), np.arange(PH), np.arange(PW), indexing="ij")
    f = (ph % 2) * 2 + pw % 2
    positions = PACK * PH * PW // 4
    rx2 = (pw // 2) % 2
    pos = ((rx2 * (PH // 2) + ph // 2) * PACK + j) * (PW // 4) + pw // 4
    table = np.zeros((PACK * PH * PW, 4 * positions), np.float32)
    table[np.arange(table.shape[0]), (f * positions + pos).ravel()] = 1.0
    return table


def field_kernel(cols, acc_ref, west_ref, east_ref, place_ref, out_ref):
    prows = out_ref.shape[0] // (PH // 4)
    channels = acc_ref.shape[1]
    wide = PACK * (PW // 4)
    rows = []
    for r in range(prows):
        for jg in range(cols // PACK):
            parts = []
            for j in range(PACK):
                col = jg * PACK + j
                v = acc_ref[r * cols + col]
                if col == 0:
                    v = v + west_ref[r].astype(F32)
                if col == cols - 1:
                    v = v + east_ref[r].astype(F32)
                parts.append(v.astype(BF16))
            rows.append(jnp.concatenate(parts, axis=1))
    moved = jnp.dot(jnp.concatenate(rows, axis=0), place_ref[...], preferred_element_type=F32)
    npos = moved.shape[1] // 4
    at = 0
    for r in range(prows):
        for jg in range(cols // PACK):
            part = moved[at : at + channels]
            at += channels
            stacked = jnp.concatenate([part[:, f * npos : (f + 1) * npos] for f in range(4)], axis=0)
            turned = stacked.astype(BF16).T
            for rx2 in range(2):
                for py in range(PH // 2):
                    start = (rx2 * (PH // 2) + py) * wide
                    lane = ((py % 2) * 2 + rx2) * 4 * channels
                    out_ref[
                        r * (PH // 4) + py // 2, jg * wide : (jg + 1) * wide, lane : lane + 4 * channels
                    ] = turned[start : start + wide]


def build_field(acc, west, east, patch_rows, patch_cols):
    _, c, pixels = acc.shape
    step = 4
    per = step * PH // 4
    place = jnp.asarray(placement(), BF16)
    return pl.pallas_call(
        functools.partial(field_kernel, patch_cols),
        grid=(patch_rows // step,),
        in_specs=[
            pl.BlockSpec((step * patch_cols, c, pixels), lambda i: (i, 0, 0)),
            pl.BlockSpec((step, c, pixels), lambda i: (i, 0, 0)),
            pl.BlockSpec((step, c, pixels), lambda i: (i, 0, 0)),
            pl.BlockSpec(place.shape, lambda i: (0, 0)),
        ],
        out_specs=pl.BlockSpec((per, patch_cols * PW // 4, 16 * c), lambda i: (i, 0, 0)),
        out_shape=jax.ShapeDtypeStruct((patch_rows * PH // 4, patch_cols * PW // 4, 16 * c), BF16),
        compiler_params=params(),
        name="field",
    )(acc, west, east, place)


def flip_lines(v, swap):
    pieces = [v[:, i : i + 128] for i in range(0, v.shape[1], 128)]
    half = len(pieces) // 2
    pieces = pieces[half:] + pieces[:half]
    if swap:
        pieces = [pltpu.roll(p, swap, 1) for p in pieces]
    return jnp.concatenate(pieces, axis=1)


def gelu(v):
    inner = np.float32(np.sqrt(2 / np.pi)) * (v + np.float32(0.044715) * (v * v * v))
    return 0.5 * v * (1.0 + jnp.tanh(inner))


def exchange_start(left, right, x_ref, col_e, col_w, send_e, send_w, recv_w, recv_e, lines, corner_w, corner_e, sems):
    nlat, nlon = lax.axis_size("lat"), lax.axis_size("lon")
    rows, cols, _ = x_ref.shape
    above = lines.shape[1]
    tile = corner_w.shape[2]
    send_sem, recv_sem = sems
    lat, lon = lax.axis_index("lat"), lax.axis_index("lon")
    is_top, is_bottom = (nlat - lat) // nlat, (lat + 1) // nlat
    west = (lat, (lon + nlon - 1) % nlon)
    east = (lat, (lon + 1) % nlon)

    def up(d):
        return (lat - 1 + is_top, (lon + is_top * (nlon // 2) + d + nlon) % nlon)

    def down(d):
        return (lat + 1 - is_bottom, (lon + is_bottom * (nlon // 2) + d + nlon) % nlon)

    barrier = pltpu.get_barrier_semaphore()
    partners = [west, east] + [up(d) for d in (-1, 0, 1)] + [down(d) for d in (-1, 0, 1)]
    for partner in partners:
        pl.semaphore_signal(barrier, inc=1, device_id=partner, device_id_type=pl.DeviceIdType.MESH)

    def body(i, _):
        for u in range(4):
            y = i * 4 + u
            v = x_ref[y, cols - tile :].astype(F32)
            for i_col in range(left):
                at = tile - left + i_col
                col_e[i_col, pl.ds(y, 1)] = v[at : at + 1]
            v = x_ref[y, :tile].astype(F32)
            for i_col in range(right):
                col_w[i_col, pl.ds(y, 1)] = v[i_col : i_col + 1]
        return 0

    lax.fori_loop(0, rows // 4, body, 0)
    send_e[...] = col_e[...].astype(BF16)
    send_w[...] = col_w[...].astype(BF16)
    pl.semaphore_wait(barrier, len(partners))

    copies = []

    def send(src, dst, slot, device):
        copy = pltpu.make_async_remote_copy(
            src_ref=src,
            dst_ref=dst,
            send_sem=send_sem.at[len(copies)],
            recv_sem=recv_sem.at[slot],
            device_id=device,
            device_id_type=pl.DeviceIdType.MESH,
        )
        copy.start()
        copies.append(copy)

    for place, y0, side in ((up, 0, 1 - is_top), (down, rows - above, is_bottom)):
        send(x_ref.at[pl.ds(y0, above)], lines.at[side], 2 + side * 3, place(0))
        send(x_ref.at[pl.ds(y0, above), pl.ds(cols - tile, tile)], corner_w.at[side], 3 + side * 3, place(1))
        send(x_ref.at[pl.ds(y0, above), pl.ds(0, tile)], corner_e.at[side], 4 + side * 3, place(-1))
    send(send_e, recv_w, 0, east)
    send(send_w, recv_e, 1, west)
    return copies


def exchange_wait(copies, recv_w, recv_e, lines, corner_w, corner_e, recv_sem):
    for slot, buffer in ((0, recv_w), (1, recv_e)):
        pltpu.make_async_copy(buffer, buffer, recv_sem.at[slot]).wait()
    for side in range(2):
        for k, buffer in enumerate((lines, corner_w, corner_e)):
            pltpu.make_async_copy(buffer.at[side], buffer.at[side], recv_sem.at[2 + side * 3 + k]).wait()
    for copy in copies:
        copy.wait_send()


def flip_lines(v, swap):
    pieces = [v[:, i : i + 128] for i in range(0, v.shape[1], 128)]
    half = len(pieces) // 2
    pieces = pieces[half:] + pieces[:half]
    if swap:
        pieces = [pltpu.roll(p, swap, 1) for p in pieces]
    return jnp.concatenate(pieces, axis=1)


def conv_kernel(
    left, right, above, below, groups, swap, taps,
    x_ref, w_ref, bias_ref, gain_ref, out_ref,
    xs, west_col, east_col, col_e, col_w, send_e, send_w, recv_w, recv_e, lines, corner_w, corner_e, send_sem, recv_sem,
):
    rows, cols, channels = x_ref.shape
    outs = w_ref.shape[1]
    tile = corner_w.shape[2]
    copies = exchange_start(
        left, right, x_ref, col_e, col_w, send_e, send_w, recv_w, recv_e, lines, corner_w, corner_e,
        (send_sem, recv_sem),
    )

    def shifted(y, line):
        xs[left, y] = line
        wide = line.astype(F32)
        for k in range(1, left + 1):
            xs[left - k, y] = pltpu.roll(wide, k, 0).astype(BF16)
        for k in range(1, right + 1):
            xs[left + k, y] = pltpu.roll(wide, cols - k, 0).astype(BF16)

    def fill(i, _):
        for u in range(2):
            y = i * 2 + u
            shifted(above + y, x_ref[y])
        return 0

    lax.fori_loop(0, rows // 2, fill, 0)
    exchange_wait(copies, recv_w, recv_e, lines, corner_w, corner_e, recv_sem)

    nlat = lax.axis_size("lat")
    lat = lax.axis_index("lat")

    def line(buffer, side, k):
        polar = lat == (0 if side == 0 else nlat - 1)
        plain = buffer[side, k].astype(F32)
        mirrored = flip_lines(buffer[side, above - 1 - k].astype(F32), swap)
        share = jnp.where(polar, 1.0, 0.0)
        return mirrored * share + plain * (1.0 - share)

    for i in range(left):
        west_col[i, pl.ds(0, rows)] = recv_w[i].astype(F32)
    for i in range(right):
        east_col[i, pl.ds(0, rows)] = recv_e[i].astype(F32)
    edge = rows
    for side, count, start in ((0, above, 0), (1, below, above + rows)):
        for k in range(count):
            shifted(start + k, line(lines, side, k).astype(BF16))
            corner = line(corner_w, side, k)
            for i in range(left):
                west_col[i, pl.ds(edge, 1)] = corner[tile - left + i : tile - left + i + 1]
            corner = line(corner_e, side, k)
            for i in range(right):
                east_col[i, pl.ds(edge, 1)] = corner[i : i + 1]
            edge += 1

    spot = lax.broadcasted_iota(jnp.int32, (tile, channels), 0)

    def patch(y, edge):
        for k in range(1, left + 1):
            v = xs[left - k, y, :tile].astype(F32)
            for i in range(k):
                v = jnp.where(spot == i, west_col[left - k + i, pl.ds(edge, 1)], v)
            xs[left - k, y, :tile] = v.astype(BF16)
        for k in range(1, right + 1):
            v = xs[left + k, y, cols - tile :].astype(F32)
            for i in range(k):
                v = jnp.where(spot == tile - k + i, east_col[i, pl.ds(edge, 1)], v)
            xs[left + k, y, cols - tile :] = v.astype(BF16)

    def patch_rows(i, _):
        for u in range(4):
            y = i * 4 + u
            patch(above + y, y)
        return 0

    lax.fori_loop(0, rows // 4, patch_rows, 0)
    for k in range(above):
        patch(k, rows + k)
    for k in range(below):
        patch(above + rows + k, rows + above + k)

    chunk = 8
    size = outs // groups
    if groups > 1:
        row = lax.broadcasted_iota(jnp.int32, (outs, outs), 0) // size
        col = lax.broadcasted_iota(jnp.int32, (outs, outs), 1) // size
        average = jnp.where(row == col, 1.0 / size, 0.0).astype(BF16)
    bias = jnp.concatenate([bias_ref[...]] * groups, axis=1)
    gain = jnp.concatenate([gain_ref[...]] * groups, axis=1)

    def body(i, _):
        y0 = i * chunk
        total = jnp.zeros((chunk * cols, outs), F32)
        at = 0
        for dy, row_taps in enumerate(taps):
            parts = []
            for dx, lanes in row_taps:
                parts.append(xs[dx, pl.ds(y0 + dy, chunk), :, lanes : lanes + 128].reshape(chunk * cols, 128))
            lhs = jnp.concatenate(parts, axis=1)
            depth = lhs.shape[1]
            total += jnp.dot(lhs, w_ref[at : at + depth], preferred_element_type=F32)
            at += depth
        total += bias
        square = total * total
        if groups > 1:
            high = square.astype(BF16)
            low = (square - high.astype(F32)).astype(BF16)
            mean = jnp.dot(high, average, preferred_element_type=F32) + jnp.dot(
                low, average, preferred_element_type=F32
            )
        else:
            mean = jnp.mean(square, axis=-1, keepdims=True)
        scaled = total * lax.rsqrt(mean + 1e-5) * gain
        out_ref[pl.ds(y0, chunk)] = gelu(scaled).astype(BF16).reshape(chunk, cols, outs)
        return 0

    lax.fori_loop(0, rows // chunk, body, 0)


def conv_block(x, weights, bias, gain, left, right, above, below, groups, swap, taps, collective_id, name):
    rows, cols, ch = x.shape
    outs = weights.shape[1]
    tile = 16
    extra = rows + 8
    vmem = pl.BlockSpec(memory_space=pltpu.VMEM)
    return pl.pallas_call(
        functools.partial(conv_kernel, left, right, above, below, groups, swap, taps),
        in_specs=[vmem] * 4,
        out_specs=vmem,
        out_shape=jax.ShapeDtypeStruct((rows, cols, outs), BF16),
        scratch_shapes=[
            pltpu.VMEM((left + right + 1, rows + above + below, cols, ch), BF16),
            pltpu.VMEM((left, extra, ch), F32),
            pltpu.VMEM((right, extra, ch), F32),
            pltpu.VMEM((left, rows, ch), F32),
            pltpu.VMEM((right, rows, ch), F32),
            pltpu.VMEM((left, rows, ch), BF16),
            pltpu.VMEM((right, rows, ch), BF16),
            pltpu.VMEM((left, rows, ch), BF16),
            pltpu.VMEM((right, rows, ch), BF16),
            pltpu.VMEM((2, above, cols, ch), BF16),
            pltpu.VMEM((2, above, tile, ch), BF16),
            pltpu.VMEM((2, above, tile, ch), BF16),
            pltpu.SemaphoreType.DMA((8,)),
            pltpu.SemaphoreType.DMA((8,)),
        ],
        compiler_params=pltpu.CompilerParams(
            collective_id=collective_id, has_side_effects=True, vmem_limit_bytes=VMEM_LIMIT
        ),
        name=name,
    )(x, weights, bias[None], gain[None])


def taps_one():
    return [
        [(dx, (ry2 * 2 + rx2) * 128) for dx in range(3) for ry2 in range(2) for rx2 in range(2)
         if not (dy == 2 and ry2) and not (dx == 2 and rx2)]
        for dy in range(3)
    ]


def taps_two():
    return [[(dx, lanes) for dx in range(4) for lanes in (0, 128)] for _ in range(4)]


def weights_one(kernel):
    _, _, ci, co = kernel.shape
    parts = []
    for sy in range(2):
        for sx in range(2):
            parts.append(jnp.pad(kernel, ((1 + 2 * sy, 4 - 2 * sy), (1 + 2 * sx, 4 - 2 * sx), (0, 0), (0, 0))))
    full = jnp.concatenate(parts, axis=-1)
    full = full.reshape(3, 2, 2, 3, 2, 2, ci, 4 * co).transpose(0, 3, 1, 4, 2, 5, 6, 7)
    full = full.reshape(9, 16 * ci, 4 * co)
    used = [full[dy * 3 + dx, lanes : lanes + 128] for dy, row in enumerate(taps_one()) for dx, lanes in row]
    return jnp.concatenate(used, axis=0)


def weights_two(kernel):
    _, _, ci, co = kernel.shape
    full = jnp.pad(kernel, ((1, 0), (1, 0), (0, 0), (0, 0)))
    return full.reshape(4, 2, 4, 2, ci, co).transpose(0, 2, 1, 3, 4, 5).reshape(16 * 4 * ci, co)


def local(
    cell_state,
    remap_weight,
    block_target,
    block_count,
    border_state,
    border_weight,
    border_target,
    kernel_one,
    bias_one,
    gain_one,
    kernel_two,
    bias_two,
    gain_two,
):
    patch_rows = TH // PH
    patch_cols = W // PW
    rim = EDGE * patch_rows
    nlon = lax.axis_size("lon")
    to_west, to_east = border_sums(border_state[0, 0], border_weight[0, 0], border_target[0, 0], 2 * rim)
    from_west = lax.ppermute(to_east, "lon", [(i, (i + 1) % nlon) for i in range(nlon)])
    from_east = lax.ppermute(to_west, "lon", [((i + 1) % nlon, i) for i in range(nlon)])
    acc = inner_sums(
        cell_state[0, 0], remap_weight[0, 0], block_target[0, 0], block_count[0], patch_rows * patch_cols
    )
    field = build_field(acc, from_west, from_east, patch_rows, patch_cols)
    one = weights_one(kernel_one)
    two = weights_two(kernel_two)
    ci = kernel_one.shape[2]
    hidden = conv_block(field, one, bias_one, gain_one, 1, 1, 1, 1, 4, 2 * ci, taps_one(), 0, "first")
    return conv_block(hidden, two, bias_two, gain_two, 2, 1, 2, 1, 1, 0, taps_two(), 1, "second")


def solution(mesh):
    placed = (
        P("lat", "lon", None, None, None),
        P("lat", "lon", None, None, None),
        P("lat", "lon", None),
        P("lat", "lon"),
        P("lat", "lon", None, None, None),
        P("lat", "lon", None, None, None),
        P("lat", "lon", None),
        P(),
        P(),
        P(),
        P(),
        P(),
        P(),
    )
    return jax.shard_map(
        local, mesh=mesh, in_specs=placed, out_specs=P("lat", "lon", None), check_vma=False
    )
```

```python
import functools

import jax
import jax.numpy as jnp
import numpy as np
from jax import lax
from jax.experimental import pallas as pl
from jax.experimental.pallas import tpu as pltpu
from jax.sharding import PartitionSpec as P

PH = 8
PW = 16
EDGE = 1
TH = 256
W = 128
PACK = 4
VMEM_LIMIT = 32 * 1024 * 1024
F32 = jnp.float32
BF16 = jnp.bfloat16


def params():
    return pltpu.CompilerParams(vmem_limit_bytes=VMEM_LIMIT)


def turn_states(s_ref, turned, distance):
    channels, _, block = s_ref.shape

    def body(i, _):
        for u in range(2):
            c = i * 2 + u
            v = s_ref[c]
            if block == distance * 2 and distance % 128 == 0:
                pair = jnp.concatenate([v[:, :distance], v[:, distance:]], axis=0)
            else:
                other = pltpu.roll(v.astype(F32), block - distance, 1).astype(BF16)
                pair = jnp.concatenate([v, other], axis=0)
            turned[pl.ds(c, distance, stride=channels)] = pair.T[:distance].astype(F32)
        return 0

    lax.fori_loop(0, channels // 2, body, 0)


def group_slots(g, distance):
    return (2 * g, 2 * g + distance, 2 * g + 1, 2 * g + 1 + distance)


def group_product(turned, w_ref, mask, g, channels, distance):
    start = pl.multiple_of(g * 2 * channels, 2 * channels)
    s = jnp.concatenate(
        [turned[pl.ds(start, channels)], turned[pl.ds(start + channels, channels)]], axis=1
    ).astype(BF16)
    lhs = jnp.concatenate([s] * PACK, axis=0) * mask
    rhs = jnp.concatenate([w_ref[slot] for slot in group_slots(g, distance)], axis=0)
    return jnp.dot(lhs, rhs, preferred_element_type=F32)


def slot_mask(channels, cells):
    row = lax.broadcasted_iota(jnp.int32, (PACK * channels, PACK * cells), 0) // channels
    col = lax.broadcasted_iota(jnp.int32, (PACK * channels, PACK * cells), 1) // cells
    return jnp.where(row == col, 1.0, 0.0).astype(BF16)


def add_groups(base, s_ref, w_ref, turned, store):
    channels, cells, block = s_ref.shape
    distance = block // 2
    turn_states(s_ref, turned, distance)
    mask = slot_mask(channels, cells)

    def body(i, _):
        prods = [group_product(turned, w_ref, mask, i * 4 + u, channels, distance) for u in range(4)]
        for u, prod in enumerate(prods):
            for k, slot in enumerate(group_slots(i * 4 + u, distance)):
                store(base + slot, prod[k * channels : (k + 1) * channels])
        return 0

    lax.fori_loop(0, block // (4 * PACK), body, 0)


def border_kernel(target_ref, s_ref, w_ref, west_ref, east_ref, acc, turned):
    acc[...] = jnp.zeros_like(acc)

    def add(slot, value):
        acc[target_ref[slot]] += value

    add_groups(0, s_ref, w_ref, turned, add)
    half = west_ref.shape[0]
    west_ref[...] = acc[:half].astype(BF16)
    east_ref[...] = acc[half:].astype(BF16)


def border_sums(states, weights, targets, count):
    n, c, b = states.shape
    pixels = weights.shape[2]
    return pl.pallas_call(
        border_kernel,
        grid_spec=pltpu.PrefetchScalarGridSpec(
            num_scalar_prefetch=1,
            grid=(1,),
            in_specs=[
                pl.BlockSpec((c, b, n), lambda i, t: (0, 0, 0)),
                pl.BlockSpec((n, b, pixels), lambda i, t: (0, 0, 0)),
            ],
            out_specs=[pl.BlockSpec((count // 2, c, pixels), lambda i, t: (0, 0, 0))] * 2,
            scratch_shapes=[pltpu.VMEM((count, c, pixels), F32), pltpu.VMEM((n // 2 * c, 2 * b), F32)],
        ),
        out_shape=[jax.ShapeDtypeStruct((count // 2, c, pixels), BF16)] * 2,
        compiler_params=params(),
        name="border_sums",
    )(targets, states.transpose(1, 2, 0), weights)


def inner_kernel(first_steps, target_ref, live_ref, s_ref, w_ref, acc, turned):
    step = pl.program_id(0)
    base = step * s_ref.shape[2]

    @pl.when(step < first_steps)
    def _():
        def put(slot, value):
            acc[target_ref[slot]] = value

        add_groups(base, s_ref, w_ref, turned, put)

    @pl.when((step >= first_steps) & (base < live_ref[0]))
    def _():
        def add(slot, value):
            alive = jnp.where(slot < live_ref[0], 1.0, 0.0)
            acc[target_ref[slot]] += value * alive

        add_groups(base, s_ref, w_ref, turned, add)


def inner_sums(states, weights, targets, live, patches):
    n, c, b = states.shape
    pixels = weights.shape[2]
    block = patches
    return pl.pallas_call(
        functools.partial(inner_kernel, patches // block),
        grid_spec=pltpu.PrefetchScalarGridSpec(
            num_scalar_prefetch=2,
            grid=(n // block,),
            in_specs=[
                pl.BlockSpec((c, b, block), lambda i, t, l: (0, 0, i)),
                pl.BlockSpec((block, b, pixels), lambda i, t, l: (i, 0, 0)),
            ],
            out_specs=pl.BlockSpec((patches, c, pixels), lambda i, t, l: (0, 0, 0)),
            scratch_shapes=[pltpu.VMEM((block // 2 * c, 2 * b), F32)],
        ),
        out_shape=jax.ShapeDtypeStruct((patches, c, pixels), F32),
        compiler_params=params(),
        name="inner_sums",
    )(targets, live, states.transpose(1, 2, 0), weights)


def placement():
    j, ph, pw = np.meshgrid(np.arange(PACK), np.arange(PH), np.arange(PW), indexing="ij")
    f = (ph % 2) * 2 + pw % 2
    positions = PACK * PH * PW // 4
    rx2 = (pw // 2) % 2
    pos = ((rx2 * (PH // 2) + ph // 2) * PACK + j) * (PW // 4) + pw // 4
    table = np.zeros((PACK * PH * PW, 4 * positions), np.float32)
    table[np.arange(table.shape[0]), (f * positions + pos).ravel()] = 1.0
    return table


def field_step(step, prows, cols, acc_ref, west_ref, east_ref, place_ref, out_ref):
    channels = acc_ref.shape[1]
    wide = PACK * (PW // 4)
    rows = []
    for r in range(prows):
        prow = step * prows + r
        for jg in range(cols // PACK):
            parts = []
            for j in range(PACK):
                col = jg * PACK + j
                v = acc_ref[prow * cols + col]
                if col == 0:
                    v = v + west_ref[prow].astype(F32)
                if col == cols - 1:
                    v = v + east_ref[prow].astype(F32)
                parts.append(v.astype(BF16))
            rows.append(jnp.concatenate(parts, axis=1))
    moved = jnp.dot(jnp.concatenate(rows, axis=0), place_ref[...], preferred_element_type=F32)
    npos = moved.shape[1] // 4
    at = 0
    for r in range(prows):
        for jg in range(cols // PACK):
            part = moved[at : at + channels]
            at += channels
            stacked = jnp.concatenate([part[:, f * npos : (f + 1) * npos] for f in range(4)], axis=0)
            turned = stacked.astype(BF16).T
            for rx2 in range(2):
                for py in range(PH // 2):
                    start = (rx2 * (PH // 2) + py) * wide
                    lane = ((py % 2) * 2 + rx2) * 4 * channels
                    out_ref[
                        (step * prows + r) * (PH // 4) + py // 2,
                        jg * wide : (jg + 1) * wide,
                        lane : lane + 4 * channels,
                    ] = turned[start : start + wide]


def gelu(v):
    inner = np.float32(np.sqrt(2 / np.pi)) * (v + np.float32(0.044715) * (v * v * v))
    return 0.5 * v * (1.0 + jnp.tanh(inner))


def positions():
    nlat, nlon = lax.axis_size("lat"), lax.axis_size("lon")
    lat, lon = lax.axis_index("lat"), lax.axis_index("lon")
    is_top, is_bottom = (nlat - lat) // nlat, (lat + 1) // nlat
    west = (lat, (lon + nlon - 1) % nlon)
    east = (lat, (lon + 1) % nlon)

    def up(d):
        return (lat - 1 + is_top, (lon + is_top * (nlon // 2) + d + nlon) % nlon)

    def down(d):
        return (lat + 1 - is_bottom, (lon + is_bottom * (nlon // 2) + d + nlon) % nlon)

    return is_top, is_bottom, west, east, up, down


def greet():
    _, _, west, east, up, down = positions()
    partners = [west, east] + [up(d) for d in (-1, 0, 1)] + [down(d) for d in (-1, 0, 1)]
    barrier = pltpu.get_barrier_semaphore()
    for partner in partners:
        pl.semaphore_signal(barrier, inc=1, device_id=partner, device_id_type=pl.DeviceIdType.MESH)
    return barrier, len(partners)


def exchange_start(left, right, greeted, x_ref, col_e, col_w, send_e, send_w, recv_w, recv_e, lines, corner_w, corner_e, sems):
    rows, cols, _ = x_ref.shape
    above = lines.shape[1]
    tile = corner_w.shape[2]
    send_sem, recv_sem = sems
    is_top, is_bottom, west, east, up, down = positions()

    def body(i, _):
        for u in range(4):
            y = i * 4 + u
            v = x_ref[y, cols - tile :].astype(F32)
            for i_col in range(left):
                at = tile - left + i_col
                col_e[i_col, pl.ds(y, 1)] = v[at : at + 1]
            v = x_ref[y, :tile].astype(F32)
            for i_col in range(right):
                col_w[i_col, pl.ds(y, 1)] = v[i_col : i_col + 1]
        return 0

    lax.fori_loop(0, rows // 4, body, 0)
    send_e[...] = col_e[...].astype(BF16)
    send_w[...] = col_w[...].astype(BF16)
    if greeted is not None:
        pl.semaphore_wait(*greeted)

    copies = []

    def send(src, dst, slot, device):
        copy = pltpu.make_async_remote_copy(
            src_ref=src,
            dst_ref=dst,
            send_sem=send_sem.at[len(copies)],
            recv_sem=recv_sem.at[slot],
            device_id=device,
            device_id_type=pl.DeviceIdType.MESH,
        )
        copy.start()
        copies.append(copy)

    for place, y0, side in ((up, 0, 1 - is_top), (down, rows - above, is_bottom)):
        send(x_ref.at[pl.ds(y0, above)], lines.at[side], 2 + side * 3, place(0))
        send(x_ref.at[pl.ds(y0, above), pl.ds(cols - tile, tile)], corner_w.at[side], 3 + side * 3, place(1))
        send(x_ref.at[pl.ds(y0, above), pl.ds(0, tile)], corner_e.at[side], 4 + side * 3, place(-1))
    send(send_e, recv_w, 0, east)
    send(send_w, recv_e, 1, west)
    return copies


def exchange_wait(copies, recv_w, recv_e, lines, corner_w, corner_e, recv_sem):
    for slot, buffer in ((0, recv_w), (1, recv_e)):
        pltpu.make_async_copy(buffer, buffer, recv_sem.at[slot]).wait()
    for side in range(2):
        for k, buffer in enumerate((lines, corner_w, corner_e)):
            pltpu.make_async_copy(buffer.at[side], buffer.at[side], recv_sem.at[2 + side * 3 + k]).wait()
    for copy in copies:
        copy.wait_send()


def flip_lines(v, swap):
    pieces = [v[:, i : i + 128] for i in range(0, v.shape[1], 128)]
    half = len(pieces) // 2
    pieces = pieces[half:] + pieces[:half]
    if swap:
        pieces = [pltpu.roll(p, swap, 1) for p in pieces]
    return jnp.concatenate(pieces, axis=1)


def conv_layer(
    left, right, above, below, groups, swap, taps, greeted,
    x_ref, w_ref, bias_ref, gain_ref, out_ref,
    xs, west_col, east_col, col_e, col_w, send_e, send_w, recv_w, recv_e, lines, corner_w, corner_e, send_sem, recv_sem,
):
    rows, cols, channels = x_ref.shape
    outs = w_ref.shape[1]
    tile = corner_w.shape[2]
    copies = exchange_start(
        left, right, greeted, x_ref, col_e, col_w, send_e, send_w, recv_w, recv_e, lines, corner_w, corner_e,
        (send_sem, recv_sem),
    )

    def shifted(y, line):
        xs[left, y] = line
        wide = line.astype(F32)
        for k in range(1, left + 1):
            xs[left - k, y] = pltpu.roll(wide, k, 0).astype(BF16)
        for k in range(1, right + 1):
            xs[left + k, y] = pltpu.roll(wide, cols - k, 0).astype(BF16)

    def fill(i, _):
        for u in range(2):
            y = i * 2 + u
            shifted(above + y, x_ref[y])
        return 0

    lax.fori_loop(0, rows // 2, fill, 0)
    exchange_wait(copies, recv_w, recv_e, lines, corner_w, corner_e, recv_sem)

    nlat = lax.axis_size("lat")
    lat = lax.axis_index("lat")

    def line(buffer, side, k):
        polar = lat == (0 if side == 0 else nlat - 1)
        plain = buffer[side, k].astype(F32)
        mirrored = flip_lines(buffer[side, above - 1 - k].astype(F32), swap)
        share = jnp.where(polar, 1.0, 0.0)
        return mirrored * share + plain * (1.0 - share)

    for i in range(left):
        west_col[i, pl.ds(0, rows)] = recv_w[i].astype(F32)
    for i in range(right):
        east_col[i, pl.ds(0, rows)] = recv_e[i].astype(F32)
    edge = rows
    for side, count, start in ((0, above, 0), (1, below, above + rows)):
        for k in range(count):
            shifted(start + k, line(lines, side, k).astype(BF16))
            corner = line(corner_w, side, k)
            for i in range(left):
                west_col[i, pl.ds(edge, 1)] = corner[tile - left + i : tile - left + i + 1]
            corner = line(corner_e, side, k)
            for i in range(right):
                east_col[i, pl.ds(edge, 1)] = corner[i : i + 1]
            edge += 1

    spot = lax.broadcasted_iota(jnp.int32, (tile, channels), 0)

    def patch(y, edge):
        for k in range(1, left + 1):
            v = xs[left - k, y, :tile].astype(F32)
            for i in range(k):
                v = jnp.where(spot == i, west_col[left - k + i, pl.ds(edge, 1)], v)
            xs[left - k, y, :tile] = v.astype(BF16)
        for k in range(1, right + 1):
            v = xs[left + k, y, cols - tile :].astype(F32)
            for i in range(k):
                v = jnp.where(spot == tile - k + i, east_col[i, pl.ds(edge, 1)], v)
            xs[left + k, y, cols - tile :] = v.astype(BF16)

    def patch_rows(i, _):
        for u in range(4):
            y = i * 4 + u
            patch(above + y, y)
        return 0

    lax.fori_loop(0, rows // 4, patch_rows, 0)
    for k in range(above):
        patch(k, rows + k)
    for k in range(below):
        patch(above + rows + k, rows + above + k)

    chunk = 8
    size = outs // groups
    if groups > 1:
        row = lax.broadcasted_iota(jnp.int32, (outs, outs), 0) // size
        col = lax.broadcasted_iota(jnp.int32, (outs, outs), 1) // size
        average = jnp.where(row == col, 1.0 / size, 0.0).astype(BF16)
    bias = jnp.concatenate([bias_ref[...]] * groups, axis=1)
    gain = jnp.concatenate([gain_ref[...]] * groups, axis=1)

    def body(i, _):
        y0 = i * chunk
        total = jnp.zeros((chunk * cols, outs), F32)
        at = 0
        for dy, row_taps in enumerate(taps):
            parts = []
            for dx, lanes in row_taps:
                parts.append(xs[dx, pl.ds(y0 + dy, chunk), :, lanes : lanes + 128].reshape(chunk * cols, 128))
            lhs = jnp.concatenate(parts, axis=1)
            depth = lhs.shape[1]
            total += jnp.dot(lhs, w_ref[at : at + depth], preferred_element_type=F32)
            at += depth
        total += bias
        square = total * total
        if groups > 1:
            high = square.astype(BF16)
            low = (square - high.astype(F32)).astype(BF16)
            mean = jnp.dot(high, average, preferred_element_type=F32) + jnp.dot(
                low, average, preferred_element_type=F32
            )
        else:
            mean = jnp.mean(square, axis=-1, keepdims=True)
        scaled = total * lax.rsqrt(mean + 1e-5) * gain
        out_ref[pl.ds(y0, chunk)] = gelu(scaled).astype(BF16).reshape(chunk, cols, outs)
        return 0

    lax.fori_loop(0, rows // chunk, body, 0)


def layer_scratch(left, right, above, below, rows, cols, ch):
    tile = 16
    return [
        pltpu.VMEM((left + right + 1, rows + above + below, cols, ch), BF16),
        pltpu.VMEM((left, rows + 8, ch), F32),
        pltpu.VMEM((right, rows + 8, ch), F32),
        pltpu.VMEM((left, rows, ch), F32),
        pltpu.VMEM((right, rows, ch), F32),
        pltpu.VMEM((left, rows, ch), BF16),
        pltpu.VMEM((right, rows, ch), BF16),
        pltpu.VMEM((left, rows, ch), BF16),
        pltpu.VMEM((right, rows, ch), BF16),
        pltpu.VMEM((2, above, cols, ch), BF16),
        pltpu.VMEM((2, above, tile, ch), BF16),
        pltpu.VMEM((2, above, tile, ch), BF16),
        pltpu.SemaphoreType.DMA((8,)),
        pltpu.SemaphoreType.DMA((8,)),
    ]


def encoder_kernel(
    patch_cols, ci,
    acc_ref, west_ref, east_ref, place_ref, w1_ref, bias1_ref, gain1_ref, w2_ref, bias2_ref, gain2_ref,
    out_ref, field, hidden, *scratch,
):
    greeted = greet()
    prows = 4
    patch_rows = west_ref.shape[0]

    def body(i, _):
        field_step(i, prows, patch_cols, acc_ref, west_ref, east_ref, place_ref, field)
        return 0

    lax.fori_loop(0, patch_rows // prows, body, 0)
    half = len(scratch) // 2
    conv_layer(
        1, 1, 1, 1, 4, 2 * ci, taps_one(), greeted,
        field, w1_ref, bias1_ref, gain1_ref, hidden, *scratch[:half],
    )
    conv_layer(
        2, 1, 2, 1, 1, 0, taps_two(), None,
        hidden, w2_ref, bias2_ref, gain2_ref, out_ref, *scratch[half:],
    )


def encode(acc, west, east, patch_rows, patch_cols, one, bias_one, gain_one, two, bias_two, gain_two):
    ci = acc.shape[1]
    rows, cols = patch_rows * PH // 4, patch_cols * PW // 4
    ch_one, ch_two, outs = 16 * ci, one.shape[1], two.shape[1]
    vmem = pl.BlockSpec(memory_space=pltpu.VMEM)
    place = jnp.asarray(placement(), BF16)
    return pl.pallas_call(
        functools.partial(encoder_kernel, patch_cols, ci),
        in_specs=[vmem] * 10,
        out_specs=vmem,
        out_shape=jax.ShapeDtypeStruct((rows, cols, outs), BF16),
        scratch_shapes=[
            pltpu.VMEM((rows, cols, ch_one), BF16),
            pltpu.VMEM((rows, cols, ch_two), BF16),
            *layer_scratch(1, 1, 1, 1, rows, cols, ch_one),
            *layer_scratch(2, 1, 2, 1, rows, cols, ch_two),
        ],
        compiler_params=pltpu.CompilerParams(
            collective_id=0, has_side_effects=True, vmem_limit_bytes=VMEM_LIMIT
        ),
        name="encoder",
    )(acc, west, east, place, one, bias_one[None], gain_one[None], two, bias_two[None], gain_two[None])


def taps_one():
    return [
        [(dx, (ry2 * 2 + rx2) * 128) for dx in range(3) for ry2 in range(2) for rx2 in range(2)
         if not (dy == 2 and ry2) and not (dx == 2 and rx2)]
        for dy in range(3)
    ]


def taps_two():
    return [[(dx, lanes) for dx in range(4) for lanes in (0, 128)] for _ in range(4)]


def weights_one(kernel):
    _, _, ci, co = kernel.shape
    parts = []
    for sy in range(2):
        for sx in range(2):
            parts.append(jnp.pad(kernel, ((1 + 2 * sy, 4 - 2 * sy), (1 + 2 * sx, 4 - 2 * sx), (0, 0), (0, 0))))
    full = jnp.concatenate(parts, axis=-1)
    full = full.reshape(3, 2, 2, 3, 2, 2, ci, 4 * co).transpose(0, 3, 1, 4, 2, 5, 6, 7)
    full = full.reshape(9, 16 * ci, 4 * co)
    used = [full[dy * 3 + dx, lanes : lanes + 128] for dy, row in enumerate(taps_one()) for dx, lanes in row]
    return jnp.concatenate(used, axis=0)


def weights_two(kernel):
    _, _, ci, co = kernel.shape
    full = jnp.pad(kernel, ((1, 0), (1, 0), (0, 0), (0, 0)))
    return full.reshape(4, 2, 4, 2, ci, co).transpose(0, 2, 1, 3, 4, 5).reshape(16 * 4 * ci, co)


def local(
    cell_state,
    remap_weight,
    block_target,
    block_count,
    border_state,
    border_weight,
    border_target,
    kernel_one,
    bias_one,
    gain_one,
    kernel_two,
    bias_two,
    gain_two,
):
    patch_rows = TH // PH
    patch_cols = W // PW
    rim = EDGE * patch_rows
    nlon = lax.axis_size("lon")
    to_west, to_east = border_sums(border_state[0, 0], border_weight[0, 0], border_target[0, 0], 2 * rim)
    from_west = lax.ppermute(to_east, "lon", [(i, (i + 1) % nlon) for i in range(nlon)])
    from_east = lax.ppermute(to_west, "lon", [((i + 1) % nlon, i) for i in range(nlon)])
    acc = inner_sums(
        cell_state[0, 0], remap_weight[0, 0], block_target[0, 0], block_count[0], patch_rows * patch_cols
    )
    one = weights_one(kernel_one)
    two = weights_two(kernel_two)
    return encode(
        acc, from_west, from_east, patch_rows, patch_cols, one, bias_one, gain_one, two, bias_two, gain_two
    )


def solution(mesh):
    placed = (
        P("lat", "lon", None, None, None),
        P("lat", "lon", None, None, None),
        P("lat", "lon", None),
        P("lat", "lon"),
        P("lat", "lon", None, None, None),
        P("lat", "lon", None, None, None),
        P("lat", "lon", None),
        P(),
        P(),
        P(),
        P(),
        P(),
        P(),
    )
    return jax.shard_map(
        local, mesh=mesh, in_specs=placed, out_specs=P("lat", "lon", None), check_vma=False
    )
```

```python
import functools

import jax
import jax.numpy as jnp
import numpy as np
from jax import lax
from jax.experimental import pallas as pl
from jax.experimental.pallas import tpu as pltpu
from jax.sharding import PartitionSpec as P

PH = 8
PW = 16
EDGE = 1
TH = 256
W = 128
PACK = 4
VMEM_LIMIT = 32 * 1024 * 1024
F32 = jnp.float32
BF16 = jnp.bfloat16


def params():
    return pltpu.CompilerParams(vmem_limit_bytes=VMEM_LIMIT)


def turn(v):
    n = v.shape[1]
    row = lax.broadcasted_iota(jnp.int32, (n, n), 0)
    col = lax.broadcasted_iota(jnp.int32, (n, n), 1)
    eye = jnp.where(row == col, 1.0, 0.0).astype(BF16)
    return lax.dot_general(eye, v, (((1,), (1,)), ((), ())), preferred_element_type=F32)


def spacing(channels):
    return channels + 8


def turn_states(s_ref, turned, distance):
    channels, _, block = s_ref.shape

    def body(i, _):
        for u in range(4):
            c = i * 4 + u
            v = s_ref[c]
            if block == distance * 2 and distance % 128 == 0:
                pair = jnp.concatenate([v[:, :distance], v[:, distance:]], axis=0)
            else:
                other = pltpu.roll(v.astype(F32), block - distance, 1).astype(BF16)
                pair = jnp.concatenate([v, other], axis=0)
            turned[pl.ds(c, distance, stride=spacing(channels))] = turn(pair)[:distance]
        return 0

    lax.fori_loop(0, channels // 4, body, 0)


def group_slots(g, distance):
    return (2 * g, 2 * g + distance, 2 * g + 1, 2 * g + 1 + distance)


def group_product(turned, w_ref, mask, g, channels, distance):
    apart = spacing(channels)
    start = pl.multiple_of(g * 2 * apart, 8)
    s = jnp.concatenate(
        [turned[pl.ds(start, channels)], turned[pl.ds(start + apart, channels)]], axis=1
    ).astype(BF16)
    lhs = jnp.concatenate([s] * PACK, axis=0) * mask
    rhs = jnp.concatenate([w_ref[slot] for slot in group_slots(g, distance)], axis=0)
    return jnp.dot(lhs, rhs, preferred_element_type=F32)


def slot_mask(channels, cells):
    row = lax.broadcasted_iota(jnp.int32, (PACK * channels, PACK * cells), 0) // channels
    col = lax.broadcasted_iota(jnp.int32, (PACK * channels, PACK * cells), 1) // cells
    return jnp.where(row == col, 1.0, 0.0).astype(BF16)


def add_groups(base, s_ref, w_ref, turned, store):
    channels, cells, block = s_ref.shape
    distance = block // 2
    turn_states(s_ref, turned, distance)
    mask = slot_mask(channels, cells)

    def body(i, _):
        prods = [group_product(turned, w_ref, mask, i * 4 + u, channels, distance) for u in range(4)]
        for u, prod in enumerate(prods):
            for k, slot in enumerate(group_slots(i * 4 + u, distance)):
                store(base + slot, prod[k * channels : (k + 1) * channels])
        return 0

    lax.fori_loop(0, block // (4 * PACK), body, 0)


def border_kernel(target_ref, s_ref, w_ref, west_ref, east_ref, acc, turned):
    acc[...] = jnp.zeros_like(acc)

    def add(slot, value):
        acc[target_ref[slot]] += value

    add_groups(0, s_ref, w_ref, turned, add)
    half = west_ref.shape[0]
    west_ref[...] = acc[:half].astype(BF16)
    east_ref[...] = acc[half:].astype(BF16)


def border_sums(states, weights, targets, count):
    n, c, b = states.shape
    pixels = weights.shape[2]
    return pl.pallas_call(
        border_kernel,
        grid_spec=pltpu.PrefetchScalarGridSpec(
            num_scalar_prefetch=1,
            grid=(1,),
            in_specs=[
                pl.BlockSpec((c, b, n), lambda i, t: (0, 0, 0)),
                pl.BlockSpec((n, b, pixels), lambda i, t: (0, 0, 0)),
            ],
            out_specs=[pl.BlockSpec((count // 2, c, pixels), lambda i, t: (0, 0, 0))] * 2,
            scratch_shapes=[pltpu.VMEM((count, c, pixels), F32), pltpu.VMEM((n // 2 * spacing(c), 2 * b), F32)],
        ),
        out_shape=[jax.ShapeDtypeStruct((count // 2, c, pixels), BF16)] * 2,
        compiler_params=params(),
        name="border_sums",
    )(targets, states.transpose(1, 2, 0), weights)


def inner_kernel(first_steps, target_ref, live_ref, s_ref, w_ref, acc, turned):
    step = pl.program_id(0)
    base = step * s_ref.shape[2]

    @pl.when(step < first_steps)
    def _():
        def put(slot, value):
            acc[target_ref[slot]] = value

        add_groups(base, s_ref, w_ref, turned, put)

    @pl.when((step >= first_steps) & (base < live_ref[0]))
    def _():
        def add(slot, value):
            alive = jnp.where(slot < live_ref[0], 1.0, 0.0)
            acc[target_ref[slot]] += value * alive

        add_groups(base, s_ref, w_ref, turned, add)


def inner_sums(states, weights, targets, live, patches):
    n, c, b = states.shape
    pixels = weights.shape[2]
    block = patches
    return pl.pallas_call(
        functools.partial(inner_kernel, patches // block),
        grid_spec=pltpu.PrefetchScalarGridSpec(
            num_scalar_prefetch=2,
            grid=(n // block,),
            in_specs=[
                pl.BlockSpec((c, b, block), lambda i, t, l: (0, 0, i)),
                pl.BlockSpec((block, b, pixels), lambda i, t, l: (i, 0, 0)),
            ],
            out_specs=pl.BlockSpec((patches, c, pixels), lambda i, t, l: (0, 0, 0)),
            scratch_shapes=[pltpu.VMEM((block // 2 * spacing(c), 2 * b), F32)],
        ),
        out_shape=jax.ShapeDtypeStruct((patches, c, pixels), F32),
        compiler_params=params(),
        name="inner_sums",
    )(targets, live, states.transpose(1, 2, 0), weights)


def placement():
    j, ph, pw = np.meshgrid(np.arange(PACK), np.arange(PH), np.arange(PW), indexing="ij")
    f = (ph % 2) * 2 + pw % 2
    positions = PACK * PH * PW // 4
    rx2 = (pw // 2) % 2
    pos = ((rx2 * (PH // 2) + ph // 2) * PACK + j) * (PW // 4) + pw // 4
    table = np.zeros((PACK * PH * PW, 4 * positions), np.float32)
    table[np.arange(table.shape[0]), (f * positions + pos).ravel()] = 1.0
    return table


def field_step(step, prows, cols, acc_ref, west_ref, east_ref, place_ref, out_ref):
    channels = acc_ref.shape[1]
    wide = PACK * (PW // 4)
    rows = []
    for r in range(prows):
        prow = step * prows + r
        for jg in range(cols // PACK):
            parts = []
            for j in range(PACK):
                col = jg * PACK + j
                v = acc_ref[prow * cols + col]
                if col == 0:
                    v = v + west_ref[prow].astype(F32)
                if col == cols - 1:
                    v = v + east_ref[prow].astype(F32)
                parts.append(v.astype(BF16))
            rows.append(jnp.concatenate(parts, axis=1))
    moved = jnp.dot(jnp.concatenate(rows, axis=0), place_ref[...], preferred_element_type=F32)
    npos = moved.shape[1] // 4
    at = 0
    for r in range(prows):
        for jg in range(cols // PACK):
            part = moved[at : at + channels]
            at += channels
            stacked = jnp.concatenate([part[:, f * npos : (f + 1) * npos] for f in range(4)], axis=0)
            turned = turn(stacked.astype(BF16)).astype(BF16)
            for rx2 in range(2):
                for py in range(PH // 2):
                    start = (rx2 * (PH // 2) + py) * wide
                    lane = ((py % 2) * 2 + rx2) * 4 * channels
                    out_ref[
                        (step * prows + r) * (PH // 4) + py // 2,
                        jg * wide : (jg + 1) * wide,
                        lane : lane + 4 * channels,
                    ] = turned[start : start + wide]


def gelu(v):
    inner = np.float32(np.sqrt(2 / np.pi)) * (v + np.float32(0.044715) * (v * v * v))
    return 0.5 * v * (1.0 + jnp.tanh(inner))


def positions():
    nlat, nlon = lax.axis_size("lat"), lax.axis_size("lon")
    lat, lon = lax.axis_index("lat"), lax.axis_index("lon")
    is_top, is_bottom = (nlat - lat) // nlat, (lat + 1) // nlat
    west = (lat, (lon + nlon - 1) % nlon)
    east = (lat, (lon + 1) % nlon)

    def up(d):
        return (lat - 1 + is_top, (lon + is_top * (nlon // 2) + d + nlon) % nlon)

    def down(d):
        return (lat + 1 - is_bottom, (lon + is_bottom * (nlon // 2) + d + nlon) % nlon)

    return is_top, is_bottom, west, east, up, down


def greet():
    _, _, west, east, up, down = positions()
    partners = [west, east] + [up(d) for d in (-1, 0, 1)] + [down(d) for d in (-1, 0, 1)]
    barrier = pltpu.get_barrier_semaphore()
    for partner in partners:
        pl.semaphore_signal(barrier, inc=1, device_id=partner, device_id_type=pl.DeviceIdType.MESH)
    return barrier, len(partners)


def exchange_start(left, right, greeted, x_ref, col_e, col_w, send_e, send_w, recv_w, recv_e, lines, corner_w, corner_e, sems):
    rows, cols, _ = x_ref.shape
    above = lines.shape[1]
    tile = corner_w.shape[2]
    send_sem, recv_sem = sems
    is_top, is_bottom, west, east, up, down = positions()

    def body(i, _):
        for u in range(4):
            y = i * 4 + u
            v = x_ref[y, cols - tile :].astype(F32)
            for i_col in range(left):
                at = tile - left + i_col
                col_e[i_col, pl.ds(y, 1)] = v[at : at + 1]
            v = x_ref[y, :tile].astype(F32)
            for i_col in range(right):
                col_w[i_col, pl.ds(y, 1)] = v[i_col : i_col + 1]
        return 0

    lax.fori_loop(0, rows // 4, body, 0)
    send_e[...] = col_e[...].astype(BF16)
    send_w[...] = col_w[...].astype(BF16)
    if greeted is not None:
        pl.semaphore_wait(*greeted)

    copies = []

    def send(src, dst, slot, device):
        copy = pltpu.make_async_remote_copy(
            src_ref=src,
            dst_ref=dst,
            send_sem=send_sem.at[len(copies)],
            recv_sem=recv_sem.at[slot],
            device_id=device,
            device_id_type=pl.DeviceIdType.MESH,
        )
        copy.start()
        copies.append(copy)

    for place, y0, side in ((up, 0, 1 - is_top), (down, rows - above, is_bottom)):
        send(x_ref.at[pl.ds(y0, above)], lines.at[side], 2 + side * 3, place(0))
        send(x_ref.at[pl.ds(y0, above), pl.ds(cols - tile, tile)], corner_w.at[side], 3 + side * 3, place(1))
        send(x_ref.at[pl.ds(y0, above), pl.ds(0, tile)], corner_e.at[side], 4 + side * 3, place(-1))
    send(send_e, recv_w, 0, east)
    send(send_w, recv_e, 1, west)
    return copies


def exchange_wait(copies, recv_w, recv_e, lines, corner_w, corner_e, recv_sem):
    for slot, buffer in ((0, recv_w), (1, recv_e)):
        pltpu.make_async_copy(buffer, buffer, recv_sem.at[slot]).wait()
    for side in range(2):
        for k, buffer in enumerate((lines, corner_w, corner_e)):
            pltpu.make_async_copy(buffer.at[side], buffer.at[side], recv_sem.at[2 + side * 3 + k]).wait()
    for copy in copies:
        copy.wait_send()


def flip_lines(v, swap):
    pieces = [v[:, i : i + 128] for i in range(0, v.shape[1], 128)]
    half = len(pieces) // 2
    pieces = pieces[half:] + pieces[:half]
    if swap:
        pieces = [pltpu.roll(p, swap, 1) for p in pieces]
    return jnp.concatenate(pieces, axis=1)


def conv_layer(
    left, right, above, below, groups, swap, taps, greeted,
    x_ref, w_ref, bias_ref, gain_ref, out_ref,
    xs, west_col, east_col, col_e, col_w, send_e, send_w, recv_w, recv_e, lines, corner_w, corner_e, send_sem, recv_sem,
):
    rows, cols, channels = x_ref.shape
    outs = w_ref.shape[1]
    tile = corner_w.shape[2]
    copies = exchange_start(
        left, right, greeted, x_ref, col_e, col_w, send_e, send_w, recv_w, recv_e, lines, corner_w, corner_e,
        (send_sem, recv_sem),
    )

    def shifted(y, line):
        xs[left, y] = line
        wide = line.astype(F32)
        for k in range(1, left + 1):
            xs[left - k, y] = pltpu.roll(wide, k, 0).astype(BF16)
        for k in range(1, right + 1):
            xs[left + k, y] = pltpu.roll(wide, cols - k, 0).astype(BF16)

    def fill(i, _):
        for u in range(2):
            y = i * 2 + u
            shifted(above + y, x_ref[y])
        return 0

    lax.fori_loop(0, rows // 2, fill, 0)
    exchange_wait(copies, recv_w, recv_e, lines, corner_w, corner_e, recv_sem)

    nlat = lax.axis_size("lat")
    lat = lax.axis_index("lat")

    def line(buffer, side, k):
        polar = lat == (0 if side == 0 else nlat - 1)
        plain = buffer[side, k].astype(F32)
        mirrored = flip_lines(buffer[side, above - 1 - k].astype(F32), swap)
        share = jnp.where(polar, 1.0, 0.0)
        return mirrored * share + plain * (1.0 - share)

    for i in range(left):
        west_col[i, pl.ds(0, rows)] = recv_w[i].astype(F32)
    for i in range(right):
        east_col[i, pl.ds(0, rows)] = recv_e[i].astype(F32)
    edge = rows
    for side, count, start in ((0, above, 0), (1, below, above + rows)):
        for k in range(count):
            shifted(start + k, line(lines, side, k).astype(BF16))
            corner = line(corner_w, side, k)
            for i in range(left):
                west_col[i, pl.ds(edge, 1)] = corner[tile - left + i : tile - left + i + 1]
            corner = line(corner_e, side, k)
            for i in range(right):
                east_col[i, pl.ds(edge, 1)] = corner[i : i + 1]
            edge += 1

    spot = lax.broadcasted_iota(jnp.int32, (tile, channels), 0)

    def patch(y, edge):
        for k in range(1, left + 1):
            v = xs[left - k, y, :tile].astype(F32)
            for i in range(k):
                v = jnp.where(spot == i, west_col[left - k + i, pl.ds(edge, 1)], v)
            xs[left - k, y, :tile] = v.astype(BF16)
        for k in range(1, right + 1):
            v = xs[left + k, y, cols - tile :].astype(F32)
            for i in range(k):
                v = jnp.where(spot == tile - k + i, east_col[i, pl.ds(edge, 1)], v)
            xs[left + k, y, cols - tile :] = v.astype(BF16)

    def patch_rows(i, _):
        for u in range(4):
            y = i * 4 + u
            patch(above + y, y)
        return 0

    lax.fori_loop(0, rows // 4, patch_rows, 0)
    for k in range(above):
        patch(k, rows + k)
    for k in range(below):
        patch(above + rows + k, rows + above + k)

    chunk = 8
    size = outs // groups
    if groups > 1:
        row = lax.broadcasted_iota(jnp.int32, (outs, outs), 0) // size
        col = lax.broadcasted_iota(jnp.int32, (outs, outs), 1) // size
        average = jnp.where(row == col, 1.0 / size, 0.0).astype(BF16)
    bias = jnp.concatenate([bias_ref[...]] * groups, axis=1)
    gain = jnp.concatenate([gain_ref[...]] * groups, axis=1)

    def body(i, _):
        y0 = i * chunk
        total = jnp.zeros((chunk * cols, outs), F32)
        at = 0
        for dy, row_taps in enumerate(taps):
            parts = []
            for dx, lanes in row_taps:
                parts.append(xs[dx, pl.ds(y0 + dy, chunk), :, lanes : lanes + 128].reshape(chunk * cols, 128))
            lhs = jnp.concatenate(parts, axis=1)
            depth = lhs.shape[1]
            total += jnp.dot(lhs, w_ref[at : at + depth], preferred_element_type=F32)
            at += depth
        total += bias
        square = total * total
        if groups > 1:
            high = square.astype(BF16)
            low = (square - high.astype(F32)).astype(BF16)
            mean = jnp.dot(high, average, preferred_element_type=F32) + jnp.dot(
                low, average, preferred_element_type=F32
            )
        else:
            mean = jnp.mean(square, axis=-1, keepdims=True)
        scaled = total * lax.rsqrt(mean + 1e-5) * gain
        out_ref[pl.ds(y0, chunk)] = gelu(scaled).astype(BF16).reshape(chunk, cols, outs)
        return 0

    lax.fori_loop(0, rows // chunk, body, 0)


def layer_scratch(left, right, above, below, rows, cols, ch):
    tile = 16
    return [
        pltpu.VMEM((left + right + 1, rows + above + below, cols, ch), BF16),
        pltpu.VMEM((left, rows + 8, ch), F32),
        pltpu.VMEM((right, rows + 8, ch), F32),
        pltpu.VMEM((left, rows, ch), F32),
        pltpu.VMEM((right, rows, ch), F32),
        pltpu.VMEM((left, rows, ch), BF16),
        pltpu.VMEM((right, rows, ch), BF16),
        pltpu.VMEM((left, rows, ch), BF16),
        pltpu.VMEM((right, rows, ch), BF16),
        pltpu.VMEM((2, above, cols, ch), BF16),
        pltpu.VMEM((2, above, tile, ch), BF16),
        pltpu.VMEM((2, above, tile, ch), BF16),
        pltpu.SemaphoreType.DMA((8,)),
        pltpu.SemaphoreType.DMA((8,)),
    ]


def encoder_kernel(
    patch_cols, ci,
    acc_ref, west_ref, east_ref, place_ref, w1_ref, bias1_ref, gain1_ref, w2_ref, bias2_ref, gain2_ref,
    out_ref, field, hidden, *scratch,
):
    greeted = greet()
    prows = 4
    patch_rows = west_ref.shape[0]

    def body(i, _):
        field_step(i, prows, patch_cols, acc_ref, west_ref, east_ref, place_ref, field)
        return 0

    lax.fori_loop(0, patch_rows // prows, body, 0)
    half = len(scratch) // 2
    conv_layer(
        1, 1, 1, 1, 4, 2 * ci, taps_one(), greeted,
        field, w1_ref, bias1_ref, gain1_ref, hidden, *scratch[:half],
    )
    conv_layer(
        2, 1, 2, 1, 1, 0, taps_two(), None,
        hidden, w2_ref, bias2_ref, gain2_ref, out_ref, *scratch[half:],
    )


def encode(acc, west, east, patch_rows, patch_cols, one, bias_one, gain_one, two, bias_two, gain_two):
    ci = acc.shape[1]
    rows, cols = patch_rows * PH // 4, patch_cols * PW // 4
    ch_one, ch_two, outs = 16 * ci, one.shape[1], two.shape[1]
    vmem = pl.BlockSpec(memory_space=pltpu.VMEM)
    place = jnp.asarray(placement(), BF16)
    return pl.pallas_call(
        functools.partial(encoder_kernel, patch_cols, ci),
        in_specs=[vmem] * 10,
        out_specs=vmem,
        out_shape=jax.ShapeDtypeStruct((rows, cols, outs), BF16),
        scratch_shapes=[
            pltpu.VMEM((rows, cols, ch_one), BF16),
            pltpu.VMEM((rows, cols, ch_two), BF16),
            *layer_scratch(1, 1, 1, 1, rows, cols, ch_one),
            *layer_scratch(2, 1, 2, 1, rows, cols, ch_two),
        ],
        compiler_params=pltpu.CompilerParams(
            collective_id=0, has_side_effects=True, vmem_limit_bytes=VMEM_LIMIT
        ),
        name="encoder",
    )(acc, west, east, place, one, bias_one[None], gain_one[None], two, bias_two[None], gain_two[None])


def taps_one():
    return [
        [(dx, (ry2 * 2 + rx2) * 128) for dx in range(3) for ry2 in range(2) for rx2 in range(2)
         if not (dy == 2 and ry2) and not (dx == 2 and rx2)]
        for dy in range(3)
    ]


def taps_two():
    return [[(dx, lanes) for dx in range(4) for lanes in (0, 128)] for _ in range(4)]


def weights_one(kernel):
    _, _, ci, co = kernel.shape
    parts = []
    for sy in range(2):
        for sx in range(2):
            parts.append(jnp.pad(kernel, ((1 + 2 * sy, 4 - 2 * sy), (1 + 2 * sx, 4 - 2 * sx), (0, 0), (0, 0))))
    full = jnp.concatenate(parts, axis=-1)
    full = full.reshape(3, 2, 2, 3, 2, 2, ci, 4 * co).transpose(0, 3, 1, 4, 2, 5, 6, 7)
    full = full.reshape(9, 16 * ci, 4 * co)
    used = [full[dy * 3 + dx, lanes : lanes + 128] for dy, row in enumerate(taps_one()) for dx, lanes in row]
    return jnp.concatenate(used, axis=0)


def weights_two(kernel):
    _, _, ci, co = kernel.shape
    full = jnp.pad(kernel, ((1, 0), (1, 0), (0, 0), (0, 0)))
    return full.reshape(4, 2, 4, 2, ci, co).transpose(0, 2, 1, 3, 4, 5).reshape(16 * 4 * ci, co)


def local(
    cell_state,
    remap_weight,
    block_target,
    block_count,
    border_state,
    border_weight,
    border_target,
    kernel_one,
    bias_one,
    gain_one,
    kernel_two,
    bias_two,
    gain_two,
):
    patch_rows = TH // PH
    patch_cols = W // PW
    rim = EDGE * patch_rows
    nlon = lax.axis_size("lon")
    to_west, to_east = border_sums(border_state[0, 0], border_weight[0, 0], border_target[0, 0], 2 * rim)
    from_west = lax.ppermute(to_east, "lon", [(i, (i + 1) % nlon) for i in range(nlon)])
    from_east = lax.ppermute(to_west, "lon", [((i + 1) % nlon, i) for i in range(nlon)])
    acc = inner_sums(
        cell_state[0, 0], remap_weight[0, 0], block_target[0, 0], block_count[0], patch_rows * patch_cols
    )
    one = weights_one(kernel_one)
    two = weights_two(kernel_two)
    return encode(
        acc, from_west, from_east, patch_rows, patch_cols, one, bias_one, gain_one, two, bias_two, gain_two
    )


def solution(mesh):
    placed = (
        P("lat", "lon", None, None, None),
        P("lat", "lon", None, None, None),
        P("lat", "lon", None),
        P("lat", "lon"),
        P("lat", "lon", None, None, None),
        P("lat", "lon", None, None, None),
        P("lat", "lon", None),
        P(),
        P(),
        P(),
        P(),
        P(),
        P(),
    )
    return jax.shard_map(
        local, mesh=mesh, in_specs=placed, out_specs=P("lat", "lon", None), check_vma=False
    )
```

```python
import functools

import jax
import jax.numpy as jnp
import numpy as np
from jax import lax
from jax.experimental import pallas as pl
from jax.experimental.pallas import tpu as pltpu
from jax.sharding import PartitionSpec as P

PH = 8
PW = 16
EDGE = 1
TH = 256
W = 128
PACK = 4
VMEM_LIMIT = 32 * 1024 * 1024
F32 = jnp.float32
BF16 = jnp.bfloat16


def params():
    return pltpu.CompilerParams(vmem_limit_bytes=VMEM_LIMIT)


def turn(v):
    n = v.shape[1]
    row = lax.broadcasted_iota(jnp.int32, (n, n), 0)
    col = lax.broadcasted_iota(jnp.int32, (n, n), 1)
    eye = jnp.where(row == col, 1.0, 0.0).astype(BF16)
    return lax.dot_general(eye, v, (((1,), (1,)), ((), ())), preferred_element_type=F32)


def spacing(channels):
    return channels + 8


def turn_states(s_ref, turned, distance):
    channels, _, block = s_ref.shape

    def body(i, _):
        for u in range(4):
            c = i * 4 + u
            v = s_ref[c]
            if block == distance * 2 and distance % 128 == 0:
                pair = jnp.concatenate([v[:, :distance], v[:, distance:]], axis=0)
            else:
                other = pltpu.roll(v.astype(F32), block - distance, 1).astype(BF16)
                pair = jnp.concatenate([v, other], axis=0)
            turned[pl.ds(c, distance, stride=spacing(channels))] = turn(pair)[:distance]
        return 0

    lax.fori_loop(0, channels // 4, body, 0)


def group_slots(g, distance):
    return (2 * g, 2 * g + distance, 2 * g + 1, 2 * g + 1 + distance)


def group_product(turned, w_ref, mask, g, channels, distance):
    apart = spacing(channels)
    start = pl.multiple_of(g * 2 * apart, 8)
    s = jnp.concatenate(
        [turned[pl.ds(start, channels)], turned[pl.ds(start + apart, channels)]], axis=1
    ).astype(BF16)
    lhs = jnp.concatenate([s] * PACK, axis=0) * mask
    rhs = jnp.concatenate([w_ref[slot] for slot in group_slots(g, distance)], axis=0)
    return jnp.dot(lhs, rhs, preferred_element_type=F32)


def slot_mask(channels, cells):
    row = lax.broadcasted_iota(jnp.int32, (PACK * channels, PACK * cells), 0) // channels
    col = lax.broadcasted_iota(jnp.int32, (PACK * channels, PACK * cells), 1) // cells
    return jnp.where(row == col, 1.0, 0.0).astype(BF16)


def add_groups(base, s_ref, w_ref, turned, store):
    channels, cells, block = s_ref.shape
    distance = block // 2
    turn_states(s_ref, turned, distance)
    mask = slot_mask(channels, cells)

    def body(i, _):
        prods = [group_product(turned, w_ref, mask, i * 8 + u, channels, distance) for u in range(8)]
        for u, prod in enumerate(prods):
            for k, slot in enumerate(group_slots(i * 8 + u, distance)):
                store(base + slot, prod[k * channels : (k + 1) * channels])
        return 0

    lax.fori_loop(0, block // (8 * PACK), body, 0)


def border_kernel(target_ref, s_ref, w_ref, west_ref, east_ref, acc, turned):
    acc[...] = jnp.zeros_like(acc)

    def add(slot, value):
        acc[target_ref[slot]] += value

    add_groups(0, s_ref, w_ref, turned, add)
    half = west_ref.shape[0]
    west_ref[...] = acc[:half].astype(BF16)
    east_ref[...] = acc[half:].astype(BF16)


def border_sums(states, weights, targets, count):
    n, c, b = states.shape
    pixels = weights.shape[2]
    return pl.pallas_call(
        border_kernel,
        grid_spec=pltpu.PrefetchScalarGridSpec(
            num_scalar_prefetch=1,
            grid=(1,),
            in_specs=[
                pl.BlockSpec((c, b, n), lambda i, t: (0, 0, 0)),
                pl.BlockSpec((n, b, pixels), lambda i, t: (0, 0, 0)),
            ],
            out_specs=[pl.BlockSpec((count // 2, c, pixels), lambda i, t: (0, 0, 0))] * 2,
            scratch_shapes=[pltpu.VMEM((count, c, pixels), F32), pltpu.VMEM((n // 2 * spacing(c), 2 * b), F32)],
        ),
        out_shape=[jax.ShapeDtypeStruct((count // 2, c, pixels), BF16)] * 2,
        compiler_params=pltpu.CompilerParams(vmem_limit_bytes=60 * 1024 * 1024),
        name="border_sums",
    )(targets, states.transpose(1, 2, 0), weights)


def inner_kernel(first_steps, target_ref, live_ref, s_ref, w_ref, acc, turned):
    step = pl.program_id(0)
    base = step * s_ref.shape[2]

    @pl.when(step < first_steps)
    def _():
        def put(slot, value):
            acc[target_ref[slot]] = value

        add_groups(base, s_ref, w_ref, turned, put)

    @pl.when((step >= first_steps) & (base < live_ref[0]))
    def _():
        def add(slot, value):
            alive = jnp.where(slot < live_ref[0], 1.0, 0.0)
            acc[target_ref[slot]] += value * alive

        add_groups(base, s_ref, w_ref, turned, add)


def inner_sums(states, weights, targets, live, patches):
    n, c, b = states.shape
    pixels = weights.shape[2]
    block = patches
    return pl.pallas_call(
        functools.partial(inner_kernel, patches // block),
        grid_spec=pltpu.PrefetchScalarGridSpec(
            num_scalar_prefetch=2,
            grid=(n // block,),
            in_specs=[
                pl.BlockSpec((c, b, block), lambda i, t, l: (0, 0, i)),
                pl.BlockSpec((block, b, pixels), lambda i, t, l: (i, 0, 0)),
            ],
            out_specs=pl.BlockSpec((patches, c, pixels), lambda i, t, l: (0, 0, 0)),
            scratch_shapes=[pltpu.VMEM((block // 2 * spacing(c), 2 * b), F32)],
        ),
        out_shape=jax.ShapeDtypeStruct((patches, c, pixels), F32),
        compiler_params=params(),
        name="inner_sums",
    )(targets, live, states.transpose(1, 2, 0), weights)


def placement():
    j, ph, pw = np.meshgrid(np.arange(PACK), np.arange(PH), np.arange(PW), indexing="ij")
    f = (ph % 2) * 2 + pw % 2
    positions = PACK * PH * PW // 4
    rx2 = (pw // 2) % 2
    pos = ((rx2 * (PH // 2) + ph // 2) * PACK + j) * (PW // 4) + pw // 4
    table = np.zeros((PACK * PH * PW, 4 * positions), np.float32)
    table[np.arange(table.shape[0]), (f * positions + pos).ravel()] = 1.0
    return table


def field_step(step, prows, cols, acc_ref, west_ref, east_ref, place_ref, out_ref):
    channels = acc_ref.shape[1]
    wide = PACK * (PW // 4)
    rows = []
    for r in range(prows):
        prow = step * prows + r
        for jg in range(cols // PACK):
            parts = []
            for j in range(PACK):
                col = jg * PACK + j
                v = acc_ref[prow * cols + col]
                if col == 0:
                    v = v + west_ref[prow].astype(F32)
                if col == cols - 1:
                    v = v + east_ref[prow].astype(F32)
                parts.append(v.astype(BF16))
            rows.append(jnp.concatenate(parts, axis=1))
    moved = jnp.dot(jnp.concatenate(rows, axis=0), place_ref[...], preferred_element_type=F32)
    npos = moved.shape[1] // 4
    at = 0
    for r in range(prows):
        for jg in range(cols // PACK):
            part = moved[at : at + channels]
            at += channels
            stacked = jnp.concatenate([part[:, f * npos : (f + 1) * npos] for f in range(4)], axis=0)
            turned = turn(stacked.astype(BF16)).astype(BF16)
            for rx2 in range(2):
                for py in range(PH // 2):
                    start = (rx2 * (PH // 2) + py) * wide
                    lane = ((py % 2) * 2 + rx2) * 4 * channels
                    out_ref[
                        (step * prows + r) * (PH // 4) + py // 2,
                        jg * wide : (jg + 1) * wide,
                        lane : lane + 4 * channels,
                    ] = turned[start : start + wide]


def gelu(v):
    inner = np.float32(np.sqrt(2 / np.pi)) * (v + np.float32(0.044715) * (v * v * v))
    return 0.5 * v * (1.0 + jnp.tanh(inner))


def positions():
    nlat, nlon = lax.axis_size("lat"), lax.axis_size("lon")
    lat, lon = lax.axis_index("lat"), lax.axis_index("lon")
    is_top, is_bottom = (nlat - lat) // nlat, (lat + 1) // nlat
    west = (lat, (lon + nlon - 1) % nlon)
    east = (lat, (lon + 1) % nlon)

    def up(d):
        return (lat - 1 + is_top, (lon + is_top * (nlon // 2) + d + nlon) % nlon)

    def down(d):
        return (lat + 1 - is_bottom, (lon + is_bottom * (nlon // 2) + d + nlon) % nlon)

    return is_top, is_bottom, west, east, up, down


def greet():
    _, _, west, east, up, down = positions()
    partners = [west, east] + [up(d) for d in (-1, 0, 1)] + [down(d) for d in (-1, 0, 1)]
    barrier = pltpu.get_barrier_semaphore()
    for partner in partners:
        pl.semaphore_signal(barrier, inc=1, device_id=partner, device_id_type=pl.DeviceIdType.MESH)
    return barrier, len(partners)


def exchange_start(left, right, greeted, x_ref, col_e, col_w, send_e, send_w, recv_w, recv_e, lines, corner_w, corner_e, sems):
    rows, cols, _ = x_ref.shape
    above = lines.shape[1]
    tile = corner_w.shape[2]
    send_sem, recv_sem = sems
    is_top, is_bottom, west, east, up, down = positions()

    def body(i, _):
        for u in range(4):
            y = i * 4 + u
            v = x_ref[y, cols - tile :].astype(F32)
            for i_col in range(left):
                at = tile - left + i_col
                col_e[i_col, pl.ds(y, 1)] = v[at : at + 1]
            v = x_ref[y, :tile].astype(F32)
            for i_col in range(right):
                col_w[i_col, pl.ds(y, 1)] = v[i_col : i_col + 1]
        return 0

    lax.fori_loop(0, rows // 4, body, 0)
    send_e[...] = col_e[...].astype(BF16)
    send_w[...] = col_w[...].astype(BF16)
    if greeted is not None:
        pl.semaphore_wait(*greeted)

    copies = []

    def send(src, dst, slot, device):
        copy = pltpu.make_async_remote_copy(
            src_ref=src,
            dst_ref=dst,
            send_sem=send_sem.at[len(copies)],
            recv_sem=recv_sem.at[slot],
            device_id=device,
            device_id_type=pl.DeviceIdType.MESH,
        )
        copy.start()
        copies.append(copy)

    for place, y0, side in ((up, 0, 1 - is_top), (down, rows - above, is_bottom)):
        send(x_ref.at[pl.ds(y0, above)], lines.at[side], 2 + side * 3, place(0))
        send(x_ref.at[pl.ds(y0, above), pl.ds(cols - tile, tile)], corner_w.at[side], 3 + side * 3, place(1))
        send(x_ref.at[pl.ds(y0, above), pl.ds(0, tile)], corner_e.at[side], 4 + side * 3, place(-1))
    send(send_e, recv_w, 0, east)
    send(send_w, recv_e, 1, west)
    return copies


def exchange_wait(copies, recv_w, recv_e, lines, corner_w, corner_e, recv_sem):
    for slot, buffer in ((0, recv_w), (1, recv_e)):
        pltpu.make_async_copy(buffer, buffer, recv_sem.at[slot]).wait()
    for side in range(2):
        for k, buffer in enumerate((lines, corner_w, corner_e)):
            pltpu.make_async_copy(buffer.at[side], buffer.at[side], recv_sem.at[2 + side * 3 + k]).wait()
    for copy in copies:
        copy.wait_send()


def flip_lines(v, swap):
    pieces = [v[:, i : i + 128] for i in range(0, v.shape[1], 128)]
    half = len(pieces) // 2
    pieces = pieces[half:] + pieces[:half]
    if swap:
        pieces = [pltpu.roll(p, swap, 1) for p in pieces]
    return jnp.concatenate(pieces, axis=1)


def conv_layer(
    left, right, above, below, groups, swap, taps, greeted,
    x_ref, w_ref, bias_ref, gain_ref, out_ref,
    xs, west_col, east_col, col_e, col_w, send_e, send_w, recv_w, recv_e, lines, corner_w, corner_e, send_sem, recv_sem,
):
    rows, cols, channels = x_ref.shape
    outs = w_ref.shape[1]
    tile = corner_w.shape[2]
    copies = exchange_start(
        left, right, greeted, x_ref, col_e, col_w, send_e, send_w, recv_w, recv_e, lines, corner_w, corner_e,
        (send_sem, recv_sem),
    )

    def shifted(y, line):
        xs[left, y] = line
        wide = line.astype(F32)
        for k in range(1, left + 1):
            xs[left - k, y] = pltpu.roll(wide, k, 0).astype(BF16)
        for k in range(1, right + 1):
            xs[left + k, y] = pltpu.roll(wide, cols - k, 0).astype(BF16)

    def fill(i, _):
        for u in range(2):
            y = i * 2 + u
            shifted(above + y, x_ref[y])
        return 0

    lax.fori_loop(0, rows // 2, fill, 0)
    exchange_wait(copies, recv_w, recv_e, lines, corner_w, corner_e, recv_sem)

    nlat = lax.axis_size("lat")
    lat = lax.axis_index("lat")

    def line(buffer, side, k):
        polar = lat == (0 if side == 0 else nlat - 1)
        plain = buffer[side, k].astype(F32)
        mirrored = flip_lines(buffer[side, above - 1 - k].astype(F32), swap)
        share = jnp.where(polar, 1.0, 0.0)
        return mirrored * share + plain * (1.0 - share)

    for i in range(left):
        west_col[i, pl.ds(0, rows)] = recv_w[i].astype(F32)
    for i in range(right):
        east_col[i, pl.ds(0, rows)] = recv_e[i].astype(F32)
    edge = rows
    for side, count, start in ((0, above, 0), (1, below, above + rows)):
        for k in range(count):
            shifted(start + k, line(lines, side, k).astype(BF16))
            corner = line(corner_w, side, k)
            for i in range(left):
                west_col[i, pl.ds(edge, 1)] = corner[tile - left + i : tile - left + i + 1]
            corner = line(corner_e, side, k)
            for i in range(right):
                east_col[i, pl.ds(edge, 1)] = corner[i : i + 1]
            edge += 1

    spot = lax.broadcasted_iota(jnp.int32, (tile, channels), 0)

    def patch(y, edge):
        for k in range(1, left + 1):
            v = xs[left - k, y, :tile].astype(F32)
            for i in range(k):
                v = jnp.where(spot == i, west_col[left - k + i, pl.ds(edge, 1)], v)
            xs[left - k, y, :tile] = v.astype(BF16)
        for k in range(1, right + 1):
            v = xs[left + k, y, cols - tile :].astype(F32)
            for i in range(k):
                v = jnp.where(spot == tile - k + i, east_col[i, pl.ds(edge, 1)], v)
            xs[left + k, y, cols - tile :] = v.astype(BF16)

    def patch_rows(i, _):
        for u in range(4):
            y = i * 4 + u
            patch(above + y, y)
        return 0

    lax.fori_loop(0, rows // 4, patch_rows, 0)
    for k in range(above):
        patch(k, rows + k)
    for k in range(below):
        patch(above + rows + k, rows + above + k)

    chunk = 8
    size = outs // groups
    if groups > 1:
        row = lax.broadcasted_iota(jnp.int32, (outs, outs), 0) // size
        col = lax.broadcasted_iota(jnp.int32, (outs, outs), 1) // size
        average = jnp.where(row == col, 1.0 / size, 0.0).astype(BF16)
    bias = jnp.concatenate([bias_ref[...]] * groups, axis=1)
    gain = jnp.concatenate([gain_ref[...]] * groups, axis=1)

    def body(i, _):
        y0 = i * chunk
        total = jnp.zeros((chunk * cols, outs), F32)
        at = 0
        for dy, row_taps in enumerate(taps):
            parts = []
            for dx, lanes in row_taps:
                parts.append(xs[dx, pl.ds(y0 + dy, chunk), :, lanes : lanes + 128].reshape(chunk * cols, 128))
            lhs = jnp.concatenate(parts, axis=1)
            depth = lhs.shape[1]
            total += jnp.dot(lhs, w_ref[at : at + depth], preferred_element_type=F32)
            at += depth
        total += bias
        square = total * total
        if groups > 1:
            high = square.astype(BF16)
            low = (square - high.astype(F32)).astype(BF16)
            mean = jnp.dot(high, average, preferred_element_type=F32) + jnp.dot(
                low, average, preferred_element_type=F32
            )
        else:
            mean = jnp.mean(square, axis=-1, keepdims=True)
        scaled = total * lax.rsqrt(mean + 1e-5) * gain
        out_ref[pl.ds(y0, chunk)] = gelu(scaled).astype(BF16).reshape(chunk, cols, outs)
        return 0

    lax.fori_loop(0, rows // chunk, body, 0)


def layer_scratch(left, right, above, below, rows, cols, ch):
    tile = 16
    return [
        pltpu.VMEM((left + right + 1, rows + above + below, cols, ch), BF16),
        pltpu.VMEM((left, rows + 8, ch), F32),
        pltpu.VMEM((right, rows + 8, ch), F32),
        pltpu.VMEM((left, rows, ch), F32),
        pltpu.VMEM((right, rows, ch), F32),
        pltpu.VMEM((left, rows, ch), BF16),
        pltpu.VMEM((right, rows, ch), BF16),
        pltpu.VMEM((left, rows, ch), BF16),
        pltpu.VMEM((right, rows, ch), BF16),
        pltpu.VMEM((2, above, cols, ch), BF16),
        pltpu.VMEM((2, above, tile, ch), BF16),
        pltpu.VMEM((2, above, tile, ch), BF16),
        pltpu.SemaphoreType.DMA((8,)),
        pltpu.SemaphoreType.DMA((8,)),
    ]


def encoder_kernel(
    patch_cols, ci,
    acc_ref, west_ref, east_ref, place_ref, w1_ref, bias1_ref, gain1_ref, w2_ref, bias2_ref, gain2_ref,
    out_ref, field, hidden, *scratch,
):
    greeted = greet()
    prows = 4
    patch_rows = west_ref.shape[0]

    def body(i, _):
        field_step(i, prows, patch_cols, acc_ref, west_ref, east_ref, place_ref, field)
        return 0

    lax.fori_loop(0, patch_rows // prows, body, 0)
    half = len(scratch) // 2
    conv_layer(
        1, 1, 1, 1, 4, 2 * ci, taps_one(), greeted,
        field, w1_ref, bias1_ref, gain1_ref, hidden, *scratch[:half],
    )
    conv_layer(
        2, 1, 2, 1, 1, 0, taps_two(), None,
        hidden, w2_ref, bias2_ref, gain2_ref, out_ref, *scratch[half:],
    )


def encode(acc, west, east, patch_rows, patch_cols, one, bias_one, gain_one, two, bias_two, gain_two):
    ci = acc.shape[1]
    rows, cols = patch_rows * PH // 4, patch_cols * PW // 4
    ch_one, ch_two, outs = 16 * ci, one.shape[1], two.shape[1]
    vmem = pl.BlockSpec(memory_space=pltpu.VMEM)
    place = jnp.asarray(placement(), BF16)
    return pl.pallas_call(
        functools.partial(encoder_kernel, patch_cols, ci),
        in_specs=[vmem] * 10,
        out_specs=vmem,
        out_shape=jax.ShapeDtypeStruct((rows, cols, outs), BF16),
        scratch_shapes=[
            pltpu.VMEM((rows, cols, ch_one), BF16),
            pltpu.VMEM((rows, cols, ch_two), BF16),
            *layer_scratch(1, 1, 1, 1, rows, cols, ch_one),
            *layer_scratch(2, 1, 2, 1, rows, cols, ch_two),
        ],
        compiler_params=pltpu.CompilerParams(
            collective_id=0, has_side_effects=True, vmem_limit_bytes=VMEM_LIMIT
        ),
        name="encoder",
    )(acc, west, east, place, one, bias_one[None], gain_one[None], two, bias_two[None], gain_two[None])


def taps_one():
    return [
        [(dx, (ry2 * 2 + rx2) * 128) for dx in range(3) for ry2 in range(2) for rx2 in range(2)
         if not (dy == 2 and ry2) and not (dx == 2 and rx2)]
        for dy in range(3)
    ]


def taps_two():
    return [[(dx, lanes) for dx in range(4) for lanes in (0, 128)] for _ in range(4)]


def weights_one(kernel):
    _, _, ci, co = kernel.shape
    parts = []
    for sy in range(2):
        for sx in range(2):
            parts.append(jnp.pad(kernel, ((1 + 2 * sy, 4 - 2 * sy), (1 + 2 * sx, 4 - 2 * sx), (0, 0), (0, 0))))
    full = jnp.concatenate(parts, axis=-1)
    full = full.reshape(3, 2, 2, 3, 2, 2, ci, 4 * co).transpose(0, 3, 1, 4, 2, 5, 6, 7)
    full = full.reshape(9, 16 * ci, 4 * co)
    used = [full[dy * 3 + dx, lanes : lanes + 128] for dy, row in enumerate(taps_one()) for dx, lanes in row]
    return jnp.concatenate(used, axis=0)


def weights_two(kernel):
    _, _, ci, co = kernel.shape
    full = jnp.pad(kernel, ((1, 0), (1, 0), (0, 0), (0, 0)))
    return full.reshape(4, 2, 4, 2, ci, co).transpose(0, 2, 1, 3, 4, 5).reshape(16 * 4 * ci, co)


def local(
    cell_state,
    remap_weight,
    block_target,
    block_count,
    border_state,
    border_weight,
    border_target,
    kernel_one,
    bias_one,
    gain_one,
    kernel_two,
    bias_two,
    gain_two,
):
    patch_rows = TH // PH
    patch_cols = W // PW
    rim = EDGE * patch_rows
    nlon = lax.axis_size("lon")
    to_west, to_east = border_sums(border_state[0, 0], border_weight[0, 0], border_target[0, 0], 2 * rim)
    from_west = lax.ppermute(to_east, "lon", [(i, (i + 1) % nlon) for i in range(nlon)])
    from_east = lax.ppermute(to_west, "lon", [((i + 1) % nlon, i) for i in range(nlon)])
    acc = inner_sums(
        cell_state[0, 0], remap_weight[0, 0], block_target[0, 0], block_count[0], patch_rows * patch_cols
    )
    one = weights_one(kernel_one)
    two = weights_two(kernel_two)
    return encode(
        acc, from_west, from_east, patch_rows, patch_cols, one, bias_one, gain_one, two, bias_two, gain_two
    )


def solution(mesh):
    placed = (
        P("lat", "lon", None, None, None),
        P("lat", "lon", None, None, None),
        P("lat", "lon", None),
        P("lat", "lon"),
        P("lat", "lon", None, None, None),
        P("lat", "lon", None, None, None),
        P("lat", "lon", None),
        P(),
        P(),
        P(),
        P(),
        P(),
        P(),
    )
    return jax.shard_map(
        local, mesh=mesh, in_specs=placed, out_specs=P("lat", "lon", None), check_vma=False
    )
```
